32 devices in a mesh: section: 4 (over z), dp: 8 (over y, x, core).
Axes of the slice: x: 2, y: 2, z: 4, core: 2. Of those that a mesh axis runs over, the one named last changes fastest.
Arguments:
- grads: bfloat16 [4, 8, 20, 8192], P('section', 'dp'), may hold values from -6400 to 6400
- owners: int32 [4, 6], P('section'), may hold values from 0 to 7, as said below
- master: float32 [4, 8, 8, 8192], P('section', 'dp'), may hold values from -0.008 to 0.008
- moment: float32 [4, 8, 8, 8192], P('section', 'dp'), may hold values from -4 to 4
- second: float32 [4, 8, 8, 8192], P('section', 'dp'), may hold values from 0.01 to 1
- average: float32 [4, 8, 8, 8192], P('section', 'dp'), may hold values from -0.0001 to 0.0001
Outputs:
- weights: bfloat16 [4, 20, 8192], P('section')
- master_out: float32 [4, 8, 8, 8192], P('section', 'dp')
- moment_out: float32 [4, 8, 8, 8192], P('section', 'dp')
- second_out: float32 [4, 8, 8, 8192], P('section', 'dp')
- average_out: float32 [4, 8, 8, 8192], P('section', 'dp')
The draws below stay inside these ranges and needn't reach their ends.
Inputs may be any that keep to these rules, and one draw needn't show every extreme that they name: The 6 tensors of one section have 6 different owners.
All inputs are finite; a program needn't handle non-finite values.
Results may differ from the reference program's by a relative error of at most 0.012.
Values may be sent and summed in bfloat16 or wider, within the bound.
A program may use at most 64 MiB of HBM per device.

```python
import math
import jax
import jax.numpy as jnp
from jax import lax

D = 8192
LAYERS = 1
ALLROWS = 20
CAP = 8
TENSORS = 6
STEP = 10
SECTIONS = 4
N_DP = 8


def draw_grads(key, part):
    key = jax.random.fold_in(key, 11)
    first, rowkey, colkey = jax.random.split(key, 3)
    shape = (SECTIONS, N_DP, ALLROWS, D)
    section_scale = (1.0 + 2.0 * jnp.arange(SECTIONS, dtype=jnp.float32) / max(SECTIONS - 1, 1)).reshape(SECTIONS, 1, 1, 1)
    row_scale = jnp.exp(jax.random.uniform(rowkey, (SECTIONS, 1, ALLROWS, 1), jnp.float32) * math.log(10.0))
    rising = 1.0 + 2.0 * jnp.arange(D, dtype=jnp.float32) / (D - 1)
    col_scale = (jnp.exp(jax.random.uniform(colkey, (D,), jnp.float32) * math.log(10.0)) * rising).reshape(1, 1, 1, D)
    base = jax.random.truncated_normal(first, -4.0, 4.0, shape, jnp.float32)
    return (base * section_scale * row_scale * col_scale).astype(jnp.bfloat16)


def draw_owners(key, part):
    key = jax.random.fold_in(key, 7)
    section_keys = jax.random.split(key, SECTIONS)

    def pick(section_key):
        return jax.random.permutation(section_key, N_DP)[:TENSORS]
    picked = jax.vmap(pick)(section_keys)
    first_key, order_key = jax.random.split(jax.random.fold_in(key, 1))
    others = 1 + jax.random.permutation(first_key, N_DP - 2)[:TENSORS - 2]
    ends = jnp.array([N_DP - 1, 0], dtype=jnp.int32)
    leading = jax.random.permutation(order_key, jnp.concatenate([ends, others.astype(jnp.int32)]))
    picked = picked.astype(jnp.int32).at[0].set(leading)
    return picked.astype(jnp.int32)


def draw_master(key, part):
    key = jax.random.fold_in(key, 21)
    shape = (SECTIONS, N_DP, CAP, D)
    base = jax.random.truncated_normal(key, -4.0, 4.0, shape, jnp.float32)
    return (0.002 * base).astype(jnp.float32)


def draw_average(key, part):
    key = jax.random.fold_in(key, 23)
    shape = (SECTIONS, N_DP, CAP, D)
    base = jax.random.truncated_normal(key, -4.0, 4.0, shape, jnp.float32)
    return (2e-05 * base).astype(jnp.float32)


def level_of(stream_key, dims, cuts, low, top_value):
    level, own = 1.0, jax.random.fold_in(stream_key, 6)
    for dim, parts in cuts:
        steps = jnp.exp(jax.random.uniform(jax.random.fold_in(own, dim), (parts,), jnp.float32, low / len(cuts), top_value / len(cuts)))
        level = level * jnp.repeat(steps, dims[dim] // parts).reshape([-1 if axis == dim else 1 for axis in range(len(dims))])
    return level


def gaussian(rng, extent, width, most, cuts=(), kind=jnp.bfloat16):
    factor_of = level_of(rng, extent, cuts, -0.22, 0.18) if cuts else 1.0
    drawn = jax.random.normal(rng, extent, jnp.float32) * width * factor_of
    return jnp.minimum(jnp.maximum(drawn, -most), most).astype(kind)


def setup_inputs(seed: int = 0) -> dict:
    key_of = jax.random.split(jax.random.key(seed), 7)
    grads = draw_grads(jax.random.fold_in(key_of[6], 71), 0)
    owners = draw_owners(jax.random.fold_in(key_of[6], 71), 0)
    master = draw_master(jax.random.fold_in(key_of[6], 71), 0)
    moment = gaussian(key_of[3], (SECTIONS, N_DP, CAP, D), 0.3, 4.0, ((0, 4), (1, 8)), jnp.float32)
    second = jnp.clip(jnp.exp(math.log(1.0) - 4.6051702 * jax.random.uniform(key_of[4], (SECTIONS, N_DP, CAP, D), jnp.float32) ** level_of(key_of[4], (SECTIONS, N_DP, CAP, D), ((0, 4), (1, 8)), -0.2, 0.2)), 0.01, 1.0)
    average = draw_average(jax.random.fold_in(key_of[6], 71), 0)
    return dict(grads=grads, owners=owners, master=master, moment=moment, second=second, average=average)


beta_one = 0.9
beta_two = 0.95
epsilon = 1e-08
learn_rate = 0.0003
decay_rate = 0.1
average_keep = 0.999
clip_level = 0.5

def tensor_layout(all_rows, slot_rows, layers):
    layer_rows = all_rows // layers
    kv_rows = (layer_rows - 2 - 2 * slot_rows) // 2
    counts = [slot_rows, kv_rows, kv_rows, slot_rows, 1, 1]
    layout = []
    start = 0
    for layer in range(layers):
        for position, count in enumerate(counts):
            layout.append((start, count, 1.0 if position < 4 else 0.0))
            start = start + count
    return layout

def adamw(grad, master, moment, second, average, decay, factor):
    clipped = factor * grad
    moment_new = beta_one * moment + (1.0 - beta_one) * clipped
    second_new = beta_two * second + (1.0 - beta_two) * clipped * clipped
    direction = moment_new / (1.0 - beta_one ** STEP) / (jnp.sqrt(second_new / (1.0 - beta_two ** STEP)) + epsilon)
    master_new = master - learn_rate * (direction + decay_rate * decay * master)
    average_new = average_keep * average + (1.0 - average_keep) * master_new
    return (master_new, moment_new, second_new, average_new)

def reference(grads, owners, master, moment, second, average):
    layout = tensor_layout(ALLROWS, CAP, LAYERS)
    means = lax.optimization_barrier(jnp.sum(grads.astype(jnp.float32), axis=1)) / N_DP
    squares = jnp.sum(means * means)
    factor = jnp.minimum(1.0, clip_level / jnp.sqrt(squares / (SECTIONS * ALLROWS * D) + 1e-06))

    def one_section(mean, owner, master_s, moment_s, second_s, average_s):
        zero = jnp.zeros((), jnp.int32)
        bucket = jnp.zeros((N_DP, CAP, D), jnp.float32)
        used = jnp.zeros((N_DP, CAP, 1), jnp.float32)
        decay = jnp.zeros((N_DP, CAP, 1), jnp.float32)
        for tensor, (start, count, flag) in enumerate(layout):
            rows = jnp.pad(mean[start:start + count], ((0, CAP - count), (0, 0)))
            marks = (jnp.arange(CAP) < count).astype(jnp.float32).reshape(1, CAP, 1)
            where_at = (owner[tensor].astype(jnp.int32), zero, zero)
            bucket = lax.dynamic_update_slice(bucket, rows[None], where_at)
            used = lax.dynamic_update_slice(used, marks, where_at)
            decay = lax.dynamic_update_slice(decay, marks * flag, where_at)
        fresh = adamw(bucket, master_s, moment_s, second_s, average_s, decay, factor)
        olds = (master_s, moment_s, second_s, average_s)
        kept = tuple((jnp.where(used > 0.5, new_value, old_value) for new_value, old_value in zip(fresh, olds)))
        pieces = []
        for tensor, (start, count, flag) in enumerate(layout):
            block = lax.dynamic_index_in_dim(kept[0], owner[tensor].astype(jnp.int32), 0, keepdims=False)
            pieces.append(block[:count])
        weights = jnp.concatenate(pieces, axis=0).astype(jnp.bfloat16)
        return (weights, kept[0], kept[1], kept[2], kept[3])
    result = jax.vmap(one_section)(means, owners, master, moment, second, average)
    return (result[0], result[1], result[2], result[3], result[4])
```

```python
import functools

import jax
import jax.numpy as jnp
from jax import lax
from jax.experimental import pallas as pl
from jax.experimental.pallas import tpu as pltpu
from jax.sharding import PartitionSpec as P

STEP = 10


beta_one = 0.9
beta_two = 0.95
epsilon = 1e-08
learn_rate = 0.0003
decay_rate = 0.1
average_keep = 0.999
clip_level = 0.5

MESH = pl.DeviceIdType.MESH
f32 = jnp.float32
bf16 = jnp.bfloat16


def tensor_layout(all_rows, slot_rows, layers):
    layer_rows = all_rows // layers
    kv_rows = (layer_rows - 2 - 2 * slot_rows) // 2
    counts = [slot_rows, kv_rows, kv_rows, slot_rows, 1, 1]
    layout = []
    start = 0
    for layer in range(layers):
        for position, count in enumerate(counts):
            layout.append((start, count, 1.0 if position < 4 else 0.0))
            start = start + count
    return layout


def adam_master(grad, master, moment, second, decay, factor):
    clipped = factor * grad
    moment_new = beta_one * moment + (1.0 - beta_one) * clipped
    second_new = beta_two * second + (1.0 - beta_two) * clipped * clipped
    direction = (
        moment_new
        / (1.0 - beta_one**STEP)
        / (jnp.sqrt(second_new / (1.0 - beta_two**STEP)) + epsilon)
    )
    master_new = master - learn_rate * (direction + decay_rate * decay * master)
    return master_new, moment_new, second_new


def clip_factor(tile, numel):
    squares = jnp.sum(tile, keepdims=True)
    return jnp.minimum(1.0, clip_level / jnp.sqrt(squares / numel + 1e-06))


def fold(x):
    half = x.shape[1] // 2
    return jnp.concatenate([x[:, :half], x[:, half:]], axis=0).astype(bf16)


def unfold(x):
    half = x.shape[0] // 2
    return jnp.concatenate([x[:half], x[half:]], axis=1)


def exchange(
    n, ns, layout, numel,
    grads, owners, master, moment, second,
    w_out, bucket_out, sq_out,
    state, st_send, st_recv, g_recv, tot, bk_send, w_rows, q_send, q_recv, s_send, s_recv,
    local_sem, g_sems, st_sems, bk_sems, q_sems, s_sems, w_sems,
):
    me = lax.axis_index("dp")
    sec = lax.axis_index("section")
    rows, width = w_out.shape
    cw = width // n
    slot_rows = state.shape[1]
    tensors = len(layout)

    def after(d):
        return lax.rem(me + d, n)

    def before(d):
        return lax.rem(me + (n - d), n)

    def cols(index):
        return pl.ds(pl.multiple_of(index * cw, cw), cw)

    loads = [
        pltpu.make_async_copy(ref.at[0, 0], state.at[k], local_sem.at[k])
        for k, ref in enumerate((master, moment, second))
    ]
    own = pltpu.make_async_copy(grads.at[0, 0, :, cols(me)], g_recv.at[0], local_sem.at[3])
    for copy in loads:
        copy.start()
    own.start()

    barrier = pltpu.get_barrier_semaphore()
    for d in range(1, n):
        pl.semaphore_signal(barrier, inc=1, device_id={"dp": after(d)}, device_id_type=MESH)
    for e in range(1, ns):
        pl.semaphore_signal(
            barrier, inc=1, device_id={"section": lax.rem(sec + e, ns)}, device_id_type=MESH
        )
    pl.semaphore_wait(barrier, n - 1 + ns - 1)

    def remote(src, dst, sems, d, target):
        copy = pltpu.make_async_remote_copy(
            src_ref=src,
            dst_ref=dst,
            send_sem=sems.at[0, d],
            recv_sem=sems.at[1, d],
            device_id=target,
            device_id_type=MESH,
        )
        copy.start()
        return copy

    g_copies = [
        remote(grads.at[0, 0, :, cols(after(d))], g_recv.at[d], g_sems, d, {"dp": after(d)})
        for d in range(1, n)
    ]

    for copy in loads:
        copy.wait()
    st_copies = []
    for d in range(n):
        place = st_recv if d == 0 else st_send
        for k in range(3):
            place[d, 2 * slot_rows * k : 2 * slot_rows * (k + 1), :] = fold(state[k, :, cols(after(d))])
        if d:
            st_copies.append(remote(st_send.at[d], st_recv.at[d], st_sems, d, {"dp": after(d)}))

    own.wait()
    total = g_recv[0].astype(f32)
    for d, copy in zip(range(1, n), g_copies):
        copy.wait_recv()
        total = total + g_recv[d].astype(f32)
    mean = total / n
    part = jnp.zeros((slot_rows, 128), f32)
    for t, (start, count, flag) in enumerate(layout):
        piece = mean[start : start + count]
        if count < slot_rows:
            piece = jnp.concatenate([piece, jnp.zeros((slot_rows - count, cw), f32)], axis=0)
        tot[t] = piece
        for c in range(0, cw, 128):
            part = part + piece[:, c : c + 128] * piece[:, c : c + 128]
    tot[tensors] = jnp.zeros((slot_rows, cw), f32)

    q_send[...] = part
    q_copies = [
        remote(q_send, q_recv.at[d], q_sems, d, {"dp": after(d)}) for d in range(1, n)
    ]

    bk_copies = []
    for d in range(n):
        target = after(d)
        mine = jnp.int32(tensors)
        for t in range(tensors):
            mine = jnp.where(owners[0, t] == target, t, mine)
        slab = fold(tot[mine])
        if d == 0:
            bucket_out[me] = slab
        else:
            bk_send[d] = slab
            bk_copies.append(
                remote(bk_send.at[d], bucket_out.at[me], bk_sems, d, {"dp": target})
            )

    for d, copy in zip(range(1, n), q_copies):
        copy.wait_recv()
        part = part + q_recv[d]
    s_send[...] = part
    s_copies = [
        remote(s_send, s_recv.at[e], s_sems, e, {"section": lax.rem(sec + e, ns)})
        for e in range(1, ns)
    ]
    for e, copy in zip(range(1, ns), s_copies):
        copy.wait_recv()
        part = part + s_recv[e]
    sq_out[...] = part
    factor = clip_factor(part, numel)

    for copy in st_copies:
        copy.wait_recv()
    for t, (start, count, flag) in enumerate(layout):
        olds = st_recv[lax.rem(me - owners[0, t] + n, n)].astype(f32)
        old = [unfold(olds[2 * slot_rows * k : 2 * slot_rows * (k + 1)]) for k in range(3)]
        fresh, _, _ = adam_master(tot[t], old[0], old[1], old[2], flag, factor)
        w_rows[start : start + count, :] = fresh[:count]
    w_out[:, cols(me)] = w_rows[...].astype(bf16)
    w_copies = [
        remote(w_out.at[:, cols(me)], w_out.at[:, cols(me)], w_sems, d, {"dp": after(d)})
        for d in range(1, n)
    ]
    for d in range(1, n):
        there = w_out.at[:, cols(before(d))]
        pltpu.make_async_copy(there, there, w_sems.at[1, d]).wait()
        place = bucket_out.at[before(d)]
        pltpu.make_async_copy(place, place, bk_sems.at[1, d]).wait()
    for copy in g_copies + st_copies + q_copies + bk_copies + s_copies + w_copies:
        copy.wait_send()


def update(
    n, layout, numel,
    owners, master, moment, second, average, bucket, squares, w_raw,
    w_out, master_out, moment_out, second_out, average_out,
    w_sem,
):
    w_copy = pltpu.make_async_copy(w_raw, w_out.at[0], w_sem)
    w_copy.start()
    me = lax.axis_index("dp")
    slot_rows, width = master.shape[2:]
    cw = width // n
    used_rows = jnp.int32(0)
    decay = jnp.float32(0.0)
    for t, (start, count, flag) in enumerate(layout):
        mine = owners[0, t] == me
        used_rows = jnp.where(mine, count, used_rows)
        decay = jnp.where(mine, flag, decay)
    used = lax.broadcasted_iota(jnp.int32, (slot_rows, cw), 0) < used_rows
    factor = clip_factor(squares[...], numel)
    for j in range(n):
        at = (0, 0, slice(None), slice(j * cw, (j + 1) * cw))
        grad = unfold(bucket[j].astype(f32))
        fresh = adam_master(grad, master[at], moment[at], second[at], decay, factor)
        kept = [
            jnp.where(used, new, old[at]) for new, old in zip(fresh, (master, moment, second))
        ]
        master_out[at] = kept[0]
        moment_out[at] = kept[1]
        second_out[at] = kept[2]
        blended = average_keep * average[at] + (1.0 - average_keep) * kept[0]
        average_out[at] = jnp.where(used, blended, average[at])
    w_copy.wait()


def local(grads, owners, master, moment, second, average):
    rows, width = grads.shape[2:]
    slot_rows = master.shape[2]
    n = lax.axis_size("dp")
    ns = lax.axis_size("section")
    cw = width // n
    layout = tensor_layout(rows, slot_rows, owners.shape[1] // 6)
    tensors = len(layout)
    numel = ns * rows * width
    vmem = pl.BlockSpec(memory_space=pltpu.VMEM)
    smem = pl.BlockSpec(memory_space=pltpu.SMEM)
    anywhere = pl.BlockSpec(memory_space=pl.ANY)
    packed = (n, 2 * slot_rows, cw // 2)
    sems = lambda count: pltpu.SemaphoreType.DMA((2, count))
    w_raw, bucket, squares = pl.pallas_call(
        functools.partial(exchange, n, ns, layout, numel),
        out_shape=(
            jax.ShapeDtypeStruct((rows, width), bf16),
            jax.ShapeDtypeStruct(packed, bf16),
            jax.ShapeDtypeStruct((slot_rows, 128), f32),
        ),
        in_specs=[anywhere, smem, anywhere, anywhere, anywhere],
        out_specs=(vmem, vmem, vmem),
        scratch_shapes=[
            pltpu.VMEM((3, slot_rows, width), f32),
            pltpu.VMEM((n, 6 * slot_rows, cw // 2), bf16),
            pltpu.VMEM((n, 6 * slot_rows, cw // 2), bf16),
            pltpu.VMEM((n, rows, cw), bf16),
            pltpu.VMEM((tensors + 1, slot_rows, cw), f32),
            pltpu.VMEM(packed, bf16),
            pltpu.VMEM((rows, cw), f32),
            pltpu.VMEM((slot_rows, 128), f32),
            pltpu.VMEM((n, slot_rows, 128), f32),
            pltpu.VMEM((slot_rows, 128), f32),
            pltpu.VMEM((ns, slot_rows, 128), f32),
            pltpu.SemaphoreType.DMA((4,)),
            sems(n), sems(n), sems(n), sems(n), sems(ns), sems(n),
        ],
        compiler_params=pltpu.CompilerParams(
            collective_id=0, has_side_effects=True, vmem_limit_bytes=24 * 2**20
        ),
        name="exchange",
    )(grads, owners, master, moment, second)
    state = jax.ShapeDtypeStruct(master.shape, f32)
    return pl.pallas_call(
        functools.partial(update, n, layout, numel),
        out_shape=(jax.ShapeDtypeStruct((1, rows, width), bf16), state, state, state, state),
        in_specs=[smem, vmem, vmem, vmem, vmem, vmem, vmem, anywhere],
        out_specs=(anywhere, vmem, vmem, vmem, vmem),
        scratch_shapes=[pltpu.SemaphoreType.DMA],
        compiler_params=pltpu.CompilerParams(vmem_limit_bytes=24 * 2**20),
        name="update",
    )(owners, master, moment, second, average, bucket, squares, w_raw)


def solution(mesh):
    in_specs = (
        P("section", "dp", None, None),
        P("section", None),
        P("section", "dp", None, None),
        P("section", "dp", None, None),
        P("section", "dp", None, None),
        P("section", "dp", None, None),
    )
    out_specs = (
        P("section", None, None),
        P("section", "dp", None, None),
        P("section", "dp", None, None),
        P("section", "dp", None, None),
        P("section", "dp", None, None),
    )
    return jax.shard_map(local, mesh=mesh, in_specs=in_specs, out_specs=out_specs, check_vma=False)
```

```python
import functools

import jax
import jax.numpy as jnp
from jax import lax
from jax.experimental import pallas as pl
from jax.experimental.pallas import tpu as pltpu
from jax.sharding import PartitionSpec as P

STEP = 10


beta_one = 0.9
beta_two = 0.95
epsilon = 1e-08
learn_rate = 0.0003
decay_rate = 0.1
average_keep = 0.999
clip_level = 0.5

MESH = pl.DeviceIdType.MESH
f32 = jnp.float32
bf16 = jnp.bfloat16


def tensor_layout(all_rows, slot_rows, layers):
    layer_rows = all_rows // layers
    kv_rows = (layer_rows - 2 - 2 * slot_rows) // 2
    counts = [slot_rows, kv_rows, kv_rows, slot_rows, 1, 1]
    layout = []
    start = 0
    for layer in range(layers):
        for position, count in enumerate(counts):
            layout.append((start, count, 1.0 if position < 4 else 0.0))
            start = start + count
    return layout


def adam_master(grad, master, moment, second, decay, factor):
    clipped = factor * grad
    moment_new = beta_one * moment + (1.0 - beta_one) * clipped
    second_new = beta_two * second + (1.0 - beta_two) * clipped * clipped
    direction = (
        moment_new
        / (1.0 - beta_one**STEP)
        / (jnp.sqrt(second_new / (1.0 - beta_two**STEP)) + epsilon)
    )
    master_new = master - learn_rate * (direction + decay_rate * decay * master)
    return master_new, moment_new, second_new


def clip_factor(tile, numel):
    squares = jnp.sum(tile, keepdims=True)
    return jnp.minimum(1.0, clip_level / jnp.sqrt(squares / numel + 1e-06))


def fold(x):
    half = x.shape[1] // 2
    return jnp.concatenate([x[:, :half], x[:, half:]], axis=0).astype(bf16)


def unfold(x):
    half = x.shape[0] // 2
    return jnp.concatenate([x[:half], x[half:]], axis=1)


def exchange(
    n, ns, layout, numel,
    grads, owners_hbm, master, moment, second, average,
    w_out, master_out, moment_out, second_out, average_out,
    owners, state, st_send, st_recv, g_recv, tot, bk_send, bk_recv, w_rows, w_send, q_send, q_recv, s_send, s_recv,
    local_sem, g_sems, st_sems, bk_sems, q_sems, s_sems, w_sems,
):
    me = lax.axis_index("dp")
    sec = lax.axis_index("section")
    rows, width = w_out.shape
    cw = width // n
    slot_rows = state.shape[1]
    tensors = len(layout)

    def after(d):
        return lax.rem(me + d, n)

    def before(d):
        return lax.rem(me + (n - d), n)

    def cols(index):
        return pl.ds(pl.multiple_of(index * cw, cw), cw)

    loads = [
        pltpu.make_async_copy(ref.at[0, 0], state.at[k], local_sem.at[k])
        for k, ref in enumerate((master, moment, second, average))
    ]
    own = pltpu.make_async_copy(grads.at[0, 0, :, cols(me)], g_recv.at[0], local_sem.at[4])
    own_owners = pltpu.make_async_copy(owners_hbm, owners, local_sem.at[5])
    for copy in loads:
        copy.start()
    own.start()
    own_owners.start()

    barrier = pltpu.get_barrier_semaphore()
    for d in range(1, n):
        pl.semaphore_signal(barrier, inc=1, device_id={"dp": after(d)}, device_id_type=MESH)
    for e in range(1, ns):
        pl.semaphore_signal(
            barrier, inc=1, device_id={"section": lax.rem(sec + e, ns)}, device_id_type=MESH
        )
    pl.semaphore_wait(barrier, n - 1 + ns - 1)

    def remote(src, dst, sems, d, target):
        copy = pltpu.make_async_remote_copy(
            src_ref=src,
            dst_ref=dst,
            send_sem=sems.at[0, d],
            recv_sem=sems.at[1, d],
            device_id=target,
            device_id_type=MESH,
        )
        copy.start()
        return copy

    g_copies = [
        remote(grads.at[0, 0, :, cols(after(d))], g_recv.at[d], g_sems, d, {"dp": after(d)})
        for d in range(1, n)
    ]

    for copy in loads[:3]:
        copy.wait()
    for d in range(n):
        place = st_recv if d == 0 else st_send
        for k in range(3):
            place[d, 2 * slot_rows * k : 2 * slot_rows * (k + 1), :] = fold(state[k, :, cols(after(d))])
    own_owners.wait()

    own.wait()
    total = g_recv[0].astype(f32)
    for d, copy in zip(range(1, n), g_copies):
        copy.wait_recv()
        total = total + g_recv[d].astype(f32)
    mean = total / n
    part = jnp.zeros((slot_rows, 128), f32)
    for t, (start, count, flag) in enumerate(layout):
        piece = mean[start : start + count]
        if count < slot_rows:
            piece = jnp.concatenate([piece, jnp.zeros((slot_rows - count, cw), f32)], axis=0)
        tot[t] = piece
        for c in range(0, cw, 128):
            part = part + piece[:, c : c + 128] * piece[:, c : c + 128]
    tot[tensors] = jnp.zeros((slot_rows, cw), f32)

    q_send[...] = part
    q_copies = [
        remote(q_send, q_recv.at[d], q_sems, d, {"dp": after(d)}) for d in range(1, n)
    ]

    st_copies = [
        remote(st_send.at[d], st_recv.at[d], st_sems, d, {"dp": after(d)}) for d in range(1, n)
    ]

    bk_copies = []
    for d in range(n):
        target = after(d)
        mine = jnp.int32(tensors)
        for t in range(tensors):
            mine = jnp.where(owners[0, t] == target, t, mine)
        slab = fold(tot[mine])
        if d == 0:
            bk_recv[me] = slab
        else:
            bk_send[d] = slab
            bk_copies.append(
                remote(bk_send.at[d], bk_recv.at[me], bk_sems, d, {"dp": target})
            )

    for d, copy in zip(range(1, n), q_copies):
        copy.wait_recv()
        part = part + q_recv[d]
    s_send[...] = part
    s_copies = [
        remote(s_send, s_recv.at[e], s_sems, e, {"section": lax.rem(sec + e, ns)})
        for e in range(1, ns)
    ]
    for e, copy in zip(range(1, ns), s_copies):
        copy.wait_recv()
        part = part + s_recv[e]
    factor = clip_factor(part, numel)

    for copy in st_copies:
        copy.wait_recv()
    for t, (start, count, flag) in enumerate(layout):
        olds = st_recv[lax.rem(me - owners[0, t] + n, n)].astype(f32)
        old = [unfold(olds[2 * slot_rows * k : 2 * slot_rows * (k + 1)]) for k in range(3)]
        fresh, _, _ = adam_master(tot[t], old[0], old[1], old[2], flag, factor)
        w_rows[start : start + count, :] = fresh[:count]
    w_send[...] = w_rows[...].astype(bf16)
    here = w_out.at[:, cols(me)]
    w_copies = [remote(w_send, here, w_sems, d, {"dp": after(d)}) for d in range(1, n)]
    w_own = pltpu.make_async_copy(w_send, here, local_sem.at[6])
    w_own.start()

    for d in range(1, n):
        place = bk_recv.at[before(d)]
        pltpu.make_async_copy(place, place, bk_sems.at[1, d]).wait()
    loads[3].wait()
    used_rows = jnp.int32(0)
    decay = jnp.float32(0.0)
    for t, (start, count, flag) in enumerate(layout):
        mine = owners[0, t] == me
        used_rows = jnp.where(mine, count, used_rows)
        decay = jnp.where(mine, flag, decay)
    used = lax.broadcasted_iota(jnp.int32, (slot_rows, cw), 0) < used_rows
    for j in range(n):
        at = slice(j * cw, (j + 1) * cw)
        old = [state[k, :, at] for k in range(4)]
        fresh = adam_master(unfold(bk_recv[j].astype(f32)), old[0], old[1], old[2], decay, factor)
        blended = average_keep * old[3] + (1.0 - average_keep) * fresh[0]
        for k, new in enumerate(fresh + (blended,)):
            state[k, :, at] = jnp.where(used, new, old[k])
    stores = [
        pltpu.make_async_copy(state.at[k], ref.at[0, 0], local_sem.at[k])
        for k, ref in enumerate((master_out, moment_out, second_out, average_out))
    ]
    for copy in stores:
        copy.start()

    for d in range(1, n):
        there = w_out.at[:, cols(before(d))]
        pltpu.make_async_copy(there, there, w_sems.at[1, d]).wait()
    for copy in g_copies + st_copies + q_copies + bk_copies + s_copies + w_copies:
        copy.wait_send()
    for copy in stores + [w_own]:
        copy.wait()


def hand_out(*refs):
    sources, results, sems = refs[:5], refs[5:10], refs[10]
    copies = [
        pltpu.make_async_copy(source, result.at[0] if k == 0 else result, sems.at[k])
        for k, (source, result) in enumerate(zip(sources, results))
    ]
    for copy in copies:
        copy.start()
    for copy in copies:
        copy.wait()


def local(grads, owners, master, moment, second, average):
    rows, width = grads.shape[2:]
    slot_rows = master.shape[2]
    n = lax.axis_size("dp")
    ns = lax.axis_size("section")
    cw = width // n
    layout = tensor_layout(rows, slot_rows, owners.shape[1] // 6)
    tensors = len(layout)
    numel = ns * rows * width
    hbm = pl.BlockSpec(memory_space=pl.ANY)
    packed = (n, 2 * slot_rows, cw // 2)
    sems = lambda count: pltpu.SemaphoreType.DMA((2, count))
    state = jax.ShapeDtypeStruct(master.shape, f32)
    results = pl.pallas_call(
        functools.partial(exchange, n, ns, layout, numel),
        out_shape=(jax.ShapeDtypeStruct((rows, width), bf16), state, state, state, state),
        in_specs=[hbm] * 6,
        out_specs=(hbm,) * 5,
        scratch_shapes=[
            pltpu.SMEM(owners.shape, jnp.int32),
            pltpu.VMEM((4, slot_rows, width), f32),
            pltpu.VMEM((n, 6 * slot_rows, cw // 2), bf16),
            pltpu.VMEM((n, 6 * slot_rows, cw // 2), bf16),
            pltpu.VMEM((n, rows, cw), bf16),
            pltpu.VMEM((tensors + 1, slot_rows, cw), f32),
            pltpu.VMEM(packed, bf16),
            pltpu.VMEM(packed, bf16),
            pltpu.VMEM((rows, cw), f32),
            pltpu.VMEM((rows, cw), bf16),
            pltpu.VMEM((slot_rows, 128), f32),
            pltpu.VMEM((n, slot_rows, 128), f32),
            pltpu.VMEM((slot_rows, 128), f32),
            pltpu.VMEM((ns, slot_rows, 128), f32),
            pltpu.SemaphoreType.DMA((7,)),
            sems(n), sems(n), sems(n), sems(n), sems(ns), sems(n),
        ],
        compiler_params=pltpu.CompilerParams(
            collective_id=0, has_side_effects=True, vmem_limit_bytes=60 * 2**20
        ),
        name="exchange",
    )(grads, owners, master, moment, second, average)
    return pl.pallas_call(
        hand_out,
        out_shape=(jax.ShapeDtypeStruct((1, rows, width), bf16), state, state, state, state),
        in_specs=[hbm] * 5,
        out_specs=(hbm,) * 5,
        scratch_shapes=[pltpu.SemaphoreType.DMA((5,))],
        compiler_params=pltpu.CompilerParams(vmem_limit_bytes=60 * 2**20),
        name="hand_out",
    )(*results)


def solution(mesh):
    in_specs = (
        P("section", "dp", None, None),
        P("section", None),
        P("section", "dp", None, None),
        P("section", "dp", None, None),
        P("section", "dp", None, None),
        P("section", "dp", None, None),
    )
    out_specs = (
        P("section", None, None),
        P("section", "dp", None, None),
        P("section", "dp", None, None),
        P("section", "dp", None, None),
        P("section", "dp", None, None),
    )
    return jax.shard_map(local, mesh=mesh, in_specs=in_specs, out_specs=out_specs, check_vma=False)
```

```python
import functools

import jax
import jax.numpy as jnp
from jax import lax
from jax.experimental import pallas as pl
from jax.experimental.pallas import tpu as pltpu
from jax.sharding import PartitionSpec as P

STEP = 10


beta_one = 0.9
beta_two = 0.95
epsilon = 1e-08
learn_rate = 0.0003
decay_rate = 0.1
average_keep = 0.999
clip_level = 0.5

MESH = pl.DeviceIdType.MESH
f32 = jnp.float32
bf16 = jnp.bfloat16


def tensor_layout(all_rows, slot_rows, layers):
    layer_rows = all_rows // layers
    kv_rows = (layer_rows - 2 - 2 * slot_rows) // 2
    counts = [slot_rows, kv_rows, kv_rows, slot_rows, 1, 1]
    layout = []
    start = 0
    for layer in range(layers):
        for position, count in enumerate(counts):
            layout.append((start, count, 1.0 if position < 4 else 0.0))
            start = start + count
    return layout


def adam_master(grad, master, moment, second, decay, factor):
    clipped = factor * grad
    moment_new = beta_one * moment + (1.0 - beta_one) * clipped
    second_new = beta_two * second + (1.0 - beta_two) * clipped * clipped
    direction = (
        moment_new
        * (1.0 / (1.0 - beta_one**STEP))
        / (jnp.sqrt(second_new * (1.0 / (1.0 - beta_two**STEP))) + epsilon)
    )
    master_new = master - learn_rate * (direction + decay_rate * decay * master)
    return master_new, moment_new, second_new


def clip_factor(tile, numel):
    squares = jnp.sum(tile, keepdims=True)
    return jnp.minimum(1.0, clip_level / jnp.sqrt(squares / numel + 1e-06))


def fold(x):
    half = x.shape[1] // 2
    return jnp.concatenate([x[:, :half], x[:, half:]], axis=0).astype(bf16)


def unfold(x):
    half = x.shape[0] // 2
    return jnp.concatenate([x[:half], x[half:]], axis=1)


def exchange(
    n, ns, layout, numel,
    grads, owners_hbm, master, moment, second, average,
    w_out, master_out, moment_out, second_out, average_out,
    owners, state, st_send, st_recv, g_mine, g_pair, g_send, g_recv, tot, bk_send, bk_recv, w_rows, w_send, q_send, q_recv, s_send, s_recv,
    local_sem, load_sem, pair_sems, g_sems, st_sems, st2_sems, bk_sems, q_sems, s_sems, w_sems, fw_sems,
):
    me = lax.axis_index("dp")
    sec = lax.axis_index("section")
    rows, width = w_out.shape
    cw = width // n
    slot_rows = state.shape[1]
    tensors = len(layout)
    chips = n // 2
    core = lax.rem(me, 2)
    sibling = me + 1 - 2 * core

    def same_core(index, e):
        return lax.rem(index + 2 * e, n)

    def after(d):
        return lax.rem(me + d, n)

    def before(d):
        return lax.rem(me + (n - d), n)

    def cols(index):
        return pl.ds(pl.multiple_of(index * cw, cw), cw)

    loads = [
        pltpu.make_async_copy(ref.at[0, 0], state.at[k], local_sem.at[k])
        for k, ref in enumerate((master, moment, second, average))
    ]
    own_owners = pltpu.make_async_copy(owners_hbm, owners, local_sem.at[4])
    own = [
        pltpu.make_async_copy(
            grads.at[0, 0, :, cols(same_core(me, e))], g_mine.at[e], load_sem.at[e]
        )
        for e in range(chips)
    ]
    for copy in loads + own + [own_owners]:
        copy.start()

    barrier = pltpu.get_barrier_semaphore()
    for d in range(1, n):
        pl.semaphore_signal(barrier, inc=1, device_id={"dp": after(d)}, device_id_type=MESH)
    for e in range(1, ns):
        pl.semaphore_signal(
            barrier, inc=1, device_id={"section": lax.rem(sec + e, ns)}, device_id_type=MESH
        )
    for copy in loads[:3]:
        copy.wait()
    for d in range(n):
        place = st_recv if d == 0 else st_send
        for k in range(3):
            place[d, 2 * slot_rows * k : 2 * slot_rows * (k + 1), :] = fold(state[k, :, cols(after(d))])
    own_owners.wait()
    for copy in own:
        copy.wait()
    pl.semaphore_wait(barrier, n - 1 + ns - 1)

    def remote(src, dst, sems, d, target):
        copy = pltpu.make_async_remote_copy(
            src_ref=src,
            dst_ref=dst,
            send_sem=sems.at[0, d],
            recv_sem=sems.at[1, d],
            device_id=target,
            device_id_type=MESH,
        )
        copy.start()
        return copy

    pair_copies = [
        remote(
            grads.at[0, 0, :, cols(same_core(sibling, e))], g_pair.at[e], pair_sems, e, {"dp": sibling}
        )
        for e in [*range(1, chips), 0]
    ]

    first = pl.ds(0, 2 * slot_rows)
    others = pl.ds(2 * slot_rows, 4 * slot_rows)
    st_copies = [
        remote(st_send.at[d, first], st_recv.at[d, first], st_sems, d, {"dp": after(d)})
        for d in range(1, n)
    ]

    g_copies = []
    for e, copy in zip([*range(1, chips), 0], pair_copies):
        copy.wait_recv()
        pair = g_mine[e].astype(f32) + g_pair[e].astype(f32)
        if e:
            g_send[e] = pair.astype(bf16)
            g_copies.append(
                remote(g_send.at[e], g_recv.at[e], g_sems, e, {"dp": same_core(me, e)})
            )
    total = pair
    for e, copy in zip(range(1, chips), g_copies):
        copy.wait_recv()
        total = total + g_recv[e].astype(f32)
    mean = total / n
    part = jnp.zeros((slot_rows, 128), f32)
    for t, (start, count, flag) in enumerate(layout):
        piece = mean[start : start + count]
        if count < slot_rows:
            piece = jnp.concatenate([piece, jnp.zeros((slot_rows - count, cw), f32)], axis=0)
        tot[t] = piece
        for c in range(0, cw, 128):
            part = part + piece[:, c : c + 128] * piece[:, c : c + 128]
    tot[tensors] = jnp.zeros((slot_rows, cw), f32)

    q_send[...] = part
    q_copies = [
        remote(q_send, q_recv.at[d], q_sems, d, {"dp": after(d)}) for d in range(1, n)
    ]

    st_copies += [
        remote(st_send.at[d, others], st_recv.at[d, others], st2_sems, d, {"dp": after(d)})
        for d in range(1, n)
    ]

    bk_copies = []
    for d in range(n):
        target = after(d)
        mine = jnp.int32(tensors)
        for t in range(tensors):
            mine = jnp.where(owners[0, t] == target, t, mine)
        slab = fold(tot[mine])
        if d == 0:
            bk_recv[me] = slab
        else:
            bk_send[d] = slab
            bk_copies.append(
                remote(bk_send.at[d], bk_recv.at[me], bk_sems, d, {"dp": target})
            )

    for d, copy in zip(range(1, n), q_copies):
        copy.wait_recv()
        part = part + q_recv[d]
    s_send[...] = part
    s_copies = [
        remote(s_send, s_recv.at[e], s_sems, e, {"section": lax.rem(sec + e, ns)})
        for e in range(1, ns)
    ]
    for e, copy in zip(range(1, ns), s_copies):
        copy.wait_recv()
        part = part + s_recv[e]
    factor = clip_factor(part, numel)

    for copy in st_copies:
        copy.wait_recv()
    for t, (start, count, flag) in enumerate(layout):
        olds = st_recv[lax.rem(me - owners[0, t] + n, n)].astype(f32)
        old = [unfold(olds[2 * slot_rows * k : 2 * slot_rows * (k + 1)]) for k in range(3)]
        fresh, _, _ = adam_master(tot[t], old[0], old[1], old[2], flag, factor)
        w_rows[start : start + count, :] = fresh[:count]
    w_send[...] = w_rows[...].astype(bf16)
    here = w_out.at[:, cols(me)]
    w_copies = [
        remote(w_send, here, w_sems, e, {"dp": same_core(me, e)}) for e in range(1, chips)
    ]
    w_copies.append(remote(w_send, here, fw_sems, 0, {"dp": sibling}))
    w_own = pltpu.make_async_copy(w_send, here, local_sem.at[5])
    w_own.start()

    for d in range(1, n):
        place = bk_recv.at[before(d)]
        pltpu.make_async_copy(place, place, bk_sems.at[1, d]).wait()
    loads[3].wait()
    used_rows = jnp.int32(0)
    decay = jnp.float32(0.0)
    for t, (start, count, flag) in enumerate(layout):
        mine = owners[0, t] == me
        used_rows = jnp.where(mine, count, used_rows)
        decay = jnp.where(mine, flag, decay)
    used = lax.broadcasted_iota(jnp.int32, (slot_rows, cw), 0) < used_rows
    for j in range(n):
        at = slice(j * cw, (j + 1) * cw)
        old = [state[k, :, at] for k in range(4)]
        fresh = adam_master(unfold(bk_recv[j].astype(f32)), old[0], old[1], old[2], decay, factor)
        blended = average_keep * old[3] + (1.0 - average_keep) * fresh[0]
        for k, new in enumerate(fresh + (blended,)):
            state[k, :, at] = jnp.where(used, new, old[k])
    stores = [
        pltpu.make_async_copy(state.at[k], ref.at[0, 0], local_sem.at[k])
        for k, ref in enumerate((master_out, moment_out, second_out, average_out))
    ]
    for copy in stores:
        copy.start()

    for e in range(1, chips):
        there = w_out.at[:, cols(same_core(me, chips - e))]
        pltpu.make_async_copy(there, there, w_sems.at[1, e]).wait()
        w_copies.append(remote(there, there, fw_sems, e, {"dp": sibling}))
    for e in range(chips):
        there = w_out.at[:, cols(same_core(sibling, chips - e))]
        pltpu.make_async_copy(there, there, fw_sems.at[1, e]).wait()
    for copy in pair_copies + g_copies + st_copies + q_copies + bk_copies + s_copies + w_copies:
        copy.wait_send()
    for copy in stores + [w_own]:
        copy.wait()


def hand_out(*refs):
    sources, results, places, sems = refs[:5], refs[5:10], refs[10:15], refs[15]
    loads = [
        pltpu.make_async_copy(source, place, sems.at[0, k])
        for k, (source, place) in enumerate(zip(sources, places))
    ]
    for copy in loads:
        copy.start()
    stores = []
    for k, (place, result) in enumerate(zip(places, results)):
        loads[k].wait()
        stores.append(pltpu.make_async_copy(place, result.at[0] if k == 0 else result, sems.at[1, k]))
        stores[-1].start()
    for copy in stores:
        copy.wait()


def local(grads, owners, master, moment, second, average):
    rows, width = grads.shape[2:]
    slot_rows = master.shape[2]
    n = lax.axis_size("dp")
    ns = lax.axis_size("section")
    cw = width // n
    layout = tensor_layout(rows, slot_rows, owners.shape[1] // 6)
    tensors = len(layout)
    numel = ns * rows * width
    hbm = pl.BlockSpec(memory_space=pl.ANY)
    packed = (n, 2 * slot_rows, cw // 2)
    sems = lambda count: pltpu.SemaphoreType.DMA((2, count))
    state = jax.ShapeDtypeStruct(master.shape, f32)
    results = pl.pallas_call(
        functools.partial(exchange, n, ns, layout, numel),
        out_shape=(jax.ShapeDtypeStruct((rows, width), bf16), state, state, state, state),
        in_specs=[hbm] * 6,
        out_specs=(hbm,) * 5,
        scratch_shapes=[
            pltpu.SMEM(owners.shape, jnp.int32),
            pltpu.VMEM((4, slot_rows, width), f32),
            pltpu.VMEM((n, 6 * slot_rows, cw // 2), bf16),
            pltpu.VMEM((n, 6 * slot_rows, cw // 2), bf16),
            *[pltpu.VMEM((n // 2, rows, cw), bf16)] * 4,
            pltpu.VMEM((tensors + 1, slot_rows, cw), f32),
            pltpu.VMEM(packed, bf16),
            pltpu.VMEM(packed, bf16),
            pltpu.VMEM((rows, cw), f32),
            pltpu.VMEM((rows, cw), bf16),
            pltpu.VMEM((slot_rows, 128), f32),
            pltpu.VMEM((n, slot_rows, 128), f32),
            pltpu.VMEM((slot_rows, 128), f32),
            pltpu.VMEM((ns, slot_rows, 128), f32),
            pltpu.SemaphoreType.DMA((6,)),
            pltpu.SemaphoreType.DMA((n // 2,)),
            sems(n // 2), sems(n // 2), sems(n), sems(n), sems(n), sems(n), sems(ns),
            sems(n // 2), sems(n // 2),
        ],
        compiler_params=pltpu.CompilerParams(
            collective_id=0, has_side_effects=True, vmem_limit_bytes=60 * 2**20
        ),
        name="exchange",
    )(grads, owners, master, moment, second, average)
    return pl.pallas_call(
        hand_out,
        out_shape=(jax.ShapeDtypeStruct((1, rows, width), bf16), state, state, state, state),
        in_specs=[hbm] * 5,
        out_specs=(hbm,) * 5,
        scratch_shapes=[
            pltpu.VMEM((rows, width), bf16),
            *[pltpu.VMEM(master.shape, f32)] * 4,
            pltpu.SemaphoreType.DMA((2, 5)),
        ],
        compiler_params=pltpu.CompilerParams(vmem_limit_bytes=60 * 2**20),
        name="hand_out",
    )(*results)


def solution(mesh):
    in_specs = (
        P("section", "dp", None, None),
        P("section", None),
        P("section", "dp", None, None),
        P("section", "dp", None, None),
        P("section", "dp", None, None),
        P("section", "dp", None, None),
    )
    out_specs = (
        P("section", None, None),
        P("section", "dp", None, None),
        P("section", "dp", None, None),
        P("section", "dp", None, None),
        P("section", "dp", None, None),
    )
    return jax.shard_map(local, mesh=mesh, in_specs=in_specs, out_specs=out_specs, check_vma=False)
```

```python
import functools

import jax
import jax.numpy as jnp
from jax import lax
from jax.experimental import pallas as pl
from jax.experimental.pallas import tpu as pltpu
from jax.sharding import PartitionSpec as P

STEP = 10


beta_one = 0.9
beta_two = 0.95
epsilon = 1e-08
learn_rate = 0.0003
decay_rate = 0.1
average_keep = 0.999
clip_level = 0.5

MESH = pl.DeviceIdType.MESH
f32 = jnp.float32
bf16 = jnp.bfloat16


def tensor_layout(all_rows, slot_rows, layers):
    layer_rows = all_rows // layers
    kv_rows = (layer_rows - 2 - 2 * slot_rows) // 2
    counts = [slot_rows, kv_rows, kv_rows, slot_rows, 1, 1]
    layout = []
    start = 0
    for layer in range(layers):
        for position, count in enumerate(counts):
            layout.append((start, count, 1.0 if position < 4 else 0.0))
            start = start + count
    return layout


def adam_master(grad, master, moment, second, decay, factor):
    clipped = factor * grad
    moment_new = beta_one * moment + (1.0 - beta_one) * clipped
    second_new = beta_two * second + (1.0 - beta_two) * clipped * clipped
    direction = (
        moment_new
        * (1.0 / (1.0 - beta_one**STEP))
        / (jnp.sqrt(second_new * (1.0 / (1.0 - beta_two**STEP))) + epsilon)
    )
    master_new = master - learn_rate * (direction + decay_rate * decay * master)
    return master_new, moment_new, second_new


def clip_factor(tile, numel):
    squares = jnp.sum(tile, keepdims=True)
    return jnp.minimum(1.0, clip_level / jnp.sqrt(squares / numel + 1e-06))


def fold(x):
    half = x.shape[1] // 2
    return jnp.concatenate([x[:, :half], x[:, half:]], axis=0).astype(bf16)


def unfold(x):
    half = x.shape[0] // 2
    return jnp.concatenate([x[:half], x[half:]], axis=1)


def exchange(
    n, ns, layout, numel,
    grads, owners_hbm, master, moment, second, average,
    w_out, master_out, moment_out, second_out, average_out,
    owners, state, st_send, st_recv, g_mine, g_pair, g_send, g_recv, tot, bk_send, bk_recv, mean_rows, old_rows, w_send, q_send, q_recv, s_send, s_recv,
    local_sem, load_sem, pair_sems, g_sems, st_sems, st2_sems, bk_sems, q_sems, s_sems, w_sems, fw_sems,
):
    me = lax.axis_index("dp")
    sec = lax.axis_index("section")
    rows, width = w_out.shape
    cw = width // n
    slot_rows = state.shape[1]
    tensors = len(layout)
    chips = n // 2
    core = lax.rem(me, 2)
    sibling = me + 1 - 2 * core

    def same_core(index, e):
        return lax.rem(index + 2 * e, n)

    def after(d):
        return lax.rem(me + d, n)

    def before(d):
        return lax.rem(me + (n - d), n)

    def cols(index):
        return pl.ds(pl.multiple_of(index * cw, cw), cw)

    loads = [
        pltpu.make_async_copy(ref.at[0, 0], state.at[k], local_sem.at[k])
        for k, ref in enumerate((master, moment, second, average))
    ]
    own_owners = pltpu.make_async_copy(owners_hbm, owners, local_sem.at[4])
    own = [
        pltpu.make_async_copy(
            grads.at[0, 0, :, cols(same_core(me, e))], g_mine.at[e], load_sem.at[e]
        )
        for e in range(chips)
    ]
    for copy in loads + own + [own_owners]:
        copy.start()

    barrier = pltpu.get_barrier_semaphore()
    for d in range(1, n):
        pl.semaphore_signal(barrier, inc=1, device_id={"dp": after(d)}, device_id_type=MESH)
    for e in range(1, ns):
        pl.semaphore_signal(
            barrier, inc=1, device_id={"section": lax.rem(sec + e, ns)}, device_id_type=MESH
        )
    pl.semaphore_wait(barrier, n - 1 + ns - 1)

    def remote(src, dst, sems, d, target):
        copy = pltpu.make_async_remote_copy(
            src_ref=src,
            dst_ref=dst,
            send_sem=sems.at[0, d],
            recv_sem=sems.at[1, d],
            device_id=target,
            device_id_type=MESH,
        )
        copy.start()
        return copy

    pair_copies = [
        remote(
            grads.at[0, 0, :, cols(same_core(sibling, e))], g_pair.at[e], pair_sems, e, {"dp": sibling}
        )
        for e in [*range(1, chips), 0]
    ]

    first = pl.ds(0, 2 * slot_rows)
    others = pl.ds(2 * slot_rows, 4 * slot_rows)
    def pack(k):
        loads[k].wait()
        for d in range(n):
            place = st_recv if d == 0 else st_send
            place[d, 2 * slot_rows * k : 2 * slot_rows * (k + 1), :] = fold(state[k, :, cols(after(d))])

    pack(0)
    st_copies = [
        remote(st_send.at[d, first], st_recv.at[d, first], st_sems, d, {"dp": after(d)})
        for d in range(1, n)
    ]

    for copy in own:
        copy.wait()
    g_copies = []
    for e, copy in zip([*range(1, chips), 0], pair_copies):
        copy.wait_recv()
        pair = g_mine[e].astype(f32) + g_pair[e].astype(f32)
        if e:
            g_send[e] = pair.astype(bf16)
            g_copies.append(
                remote(g_send.at[e], g_recv.at[e], g_sems, e, {"dp": same_core(me, e)})
            )
    pack(1)
    pack(2)
    own_owners.wait()
    total = pair
    for e, copy in zip(range(1, chips), g_copies):
        copy.wait_recv()
        total = total + g_recv[e].astype(f32)
    mean = total / n
    mean_rows[...] = mean
    part = jnp.zeros((slot_rows, 128), f32)
    for r in range(0, rows, slot_rows):
        piece = mean[r : r + slot_rows]
        for c in range(0, cw, 128):
            square = piece[:, c : c + 128] * piece[:, c : c + 128]
            if len(square) < slot_rows:
                lacking = jnp.zeros((slot_rows - len(square), 128), f32)
                square = jnp.concatenate([square, lacking], axis=0)
            part = part + square

    q_send[...] = part
    q_copies = [
        remote(q_send, q_recv.at[d], q_sems, d, {"dp": after(d)}) for d in range(1, n)
    ]

    st_copies += [
        remote(st_send.at[d, others], st_recv.at[d, others], st2_sems, d, {"dp": after(d)})
        for d in range(1, n)
    ]

    for t, (start, count, flag) in enumerate(layout):
        piece = mean_rows[start : start + count, :]
        if count < slot_rows:
            piece = jnp.concatenate([piece, jnp.zeros((slot_rows - count, cw), f32)], axis=0)
        tot[t] = piece
    tot[tensors] = jnp.zeros((slot_rows, cw), f32)

    for d, copy in zip(range(1, n), q_copies):
        copy.wait_recv()
        part = part + q_recv[d]
    s_send[...] = part
    s_copies = [
        remote(s_send, s_recv.at[e], s_sems, e, {"section": lax.rem(sec + e, ns)})
        for e in range(1, ns)
    ]

    bk_copies = []
    for d in range(n):
        target = after(d)
        mine = jnp.int32(tensors)
        for t in range(tensors):
            mine = jnp.where(owners[0, t] == target, t, mine)
        slab = fold(tot[mine])
        if d == 0:
            bk_recv[me] = slab
        else:
            bk_send[d] = slab
            bk_copies.append(
                remote(bk_send.at[d], bk_recv.at[me], bk_sems, d, {"dp": target})
            )

    for copy in st_copies:
        copy.wait_recv()
    row = lax.broadcasted_iota(jnp.int32, (rows, cw), 0)
    decays = jnp.zeros((rows, cw), f32)
    for t, (start, count, flag) in enumerate(layout):
        olds = st_recv[lax.rem(me - owners[0, t] + n, n)].astype(f32)
        for k in range(3):
            old = unfold(olds[2 * slot_rows * k : 2 * slot_rows * (k + 1)])
            old_rows[k, start : start + count, :] = old[:count]
        if flag:
            decays = jnp.where(jnp.logical_and(row >= start, row < start + count), flag, decays)

    for e, copy in zip(range(1, ns), s_copies):
        copy.wait_recv()
        part = part + s_recv[e]
    factor = clip_factor(part, numel)
    fresh, _, _ = adam_master(mean_rows[...], old_rows[0], old_rows[1], old_rows[2], decays, factor)
    w_send[...] = fresh.astype(bf16)
    here = w_out.at[:, cols(me)]
    w_copies = [
        remote(w_send, here, w_sems, e, {"dp": same_core(me, e)}) for e in range(1, chips)
    ]
    w_copies.append(remote(w_send, here, fw_sems, 0, {"dp": sibling}))
    w_own = pltpu.make_async_copy(w_send, here, local_sem.at[5])
    w_own.start()

    for d in range(1, n):
        place = bk_recv.at[before(d)]
        pltpu.make_async_copy(place, place, bk_sems.at[1, d]).wait()
    loads[3].wait()
    used_rows = jnp.int32(0)
    decay = jnp.float32(0.0)
    for t, (start, count, flag) in enumerate(layout):
        mine = owners[0, t] == me
        used_rows = jnp.where(mine, count, used_rows)
        decay = jnp.where(mine, flag, decay)
    used = lax.broadcasted_iota(jnp.int32, (slot_rows, cw), 0) < used_rows
    for j in range(n):
        at = slice(j * cw, (j + 1) * cw)
        old = [state[k, :, at] for k in range(4)]
        fresh = adam_master(unfold(bk_recv[j].astype(f32)), old[0], old[1], old[2], decay, factor)
        blended = average_keep * old[3] + (1.0 - average_keep) * fresh[0]
        for k, new in enumerate(fresh + (blended,)):
            state[k, :, at] = jnp.where(used, new, old[k])
    stores = [
        pltpu.make_async_copy(state.at[k], ref.at[0, 0], local_sem.at[k])
        for k, ref in enumerate((master_out, moment_out, second_out, average_out))
    ]
    for copy in stores:
        copy.start()

    for copy in pair_copies + g_copies + st_copies + q_copies + s_copies + bk_copies:
        copy.wait_send()

    for e in range(1, chips):
        there = w_out.at[:, cols(same_core(me, chips - e))]
        pltpu.make_async_copy(there, there, w_sems.at[1, e]).wait()
        w_copies.append(remote(there, there, fw_sems, e, {"dp": sibling}))
    for e in range(chips):
        there = w_out.at[:, cols(same_core(sibling, chips - e))]
        pltpu.make_async_copy(there, there, fw_sems.at[1, e]).wait()
    for copy in w_copies:
        copy.wait_send()
    for copy in stores + [w_own]:
        copy.wait()


def hand_out(*refs):
    sources, results, places, sems = refs[:5], refs[5:10], refs[10:15], refs[15]
    loads = [
        pltpu.make_async_copy(source, place, sems.at[0, k])
        for k, (source, place) in enumerate(zip(sources, places))
    ]
    for copy in loads:
        copy.start()
    stores = []
    for k, (place, result) in enumerate(zip(places, results)):
        loads[k].wait()
        stores.append(pltpu.make_async_copy(place, result.at[0] if k == 0 else result, sems.at[1, k]))
        stores[-1].start()
    for copy in stores:
        copy.wait()


def local(grads, owners, master, moment, second, average):
    rows, width = grads.shape[2:]
    slot_rows = master.shape[2]
    n = lax.axis_size("dp")
    ns = lax.axis_size("section")
    cw = width // n
    layout = tensor_layout(rows, slot_rows, owners.shape[1] // 6)
    tensors = len(layout)
    numel = ns * rows * width
    hbm = pl.BlockSpec(memory_space=pl.ANY)
    packed = (n, 2 * slot_rows, cw // 2)
    sems = lambda count: pltpu.SemaphoreType.DMA((2, count))
    state = jax.ShapeDtypeStruct(master.shape, f32)
    results = pl.pallas_call(
        functools.partial(exchange, n, ns, layout, numel),
        out_shape=(jax.ShapeDtypeStruct((rows, width), bf16), state, state, state, state),
        in_specs=[hbm] * 6,
        out_specs=(hbm,) * 5,
        scratch_shapes=[
            pltpu.SMEM(owners.shape, jnp.int32),
            pltpu.VMEM((4, slot_rows, width), f32),
            pltpu.VMEM((n, 6 * slot_rows, cw // 2), bf16),
            pltpu.VMEM((n, 6 * slot_rows, cw // 2), bf16),
            *[pltpu.VMEM((n // 2, rows, cw), bf16)] * 4,
            pltpu.VMEM((tensors + 1, slot_rows, cw), f32),
            pltpu.VMEM(packed, bf16),
            pltpu.VMEM(packed, bf16),
            pltpu.VMEM((rows, cw), f32),
            pltpu.VMEM((3, rows, cw), f32),
            pltpu.VMEM((rows, cw), bf16),
            pltpu.VMEM((slot_rows, 128), f32),
            pltpu.VMEM((n, slot_rows, 128), f32),
            pltpu.VMEM((slot_rows, 128), f32),
            pltpu.VMEM((ns, slot_rows, 128), f32),
            pltpu.SemaphoreType.DMA((6,)),
            pltpu.SemaphoreType.DMA((n // 2,)),
            sems(n // 2), sems(n // 2), sems(n), sems(n), sems(n), sems(n), sems(ns),
            sems(n // 2), sems(n // 2),
        ],
        compiler_params=pltpu.CompilerParams(
            collective_id=0, has_side_effects=True, vmem_limit_bytes=60 * 2**20
        ),
        name="exchange",
    )(grads, owners, master, moment, second, average)
    return pl.pallas_call(
        hand_out,
        out_shape=(jax.ShapeDtypeStruct((1, rows, width), bf16), state, state, state, state),
        in_specs=[hbm] * 5,
        out_specs=(hbm,) * 5,
        scratch_shapes=[
            pltpu.VMEM((rows, width), bf16),
            *[pltpu.VMEM(master.shape, f32)] * 4,
            pltpu.SemaphoreType.DMA((2, 5)),
        ],
        compiler_params=pltpu.CompilerParams(vmem_limit_bytes=60 * 2**20),
        name="hand_out",
    )(*results)


def solution(mesh):
    in_specs = (
        P("section", "dp", None, None),
        P("section", None),
        P("section", "dp", None, None),
        P("section", "dp", None, None),
        P("section", "dp", None, None),
        P("section", "dp", None, None),
    )
    out_specs = (
        P("section", None, None),
        P("section", "dp", None, None),
        P("section", "dp", None, None),
        P("section", "dp", None, None),
        P("section", "dp", None, None),
    )
    return jax.shard_map(local, mesh=mesh, in_specs=in_specs, out_specs=out_specs, check_vma=False)
```

```python
import functools

import jax
import jax.numpy as jnp
from jax import lax
from jax.experimental import pallas as pl
from jax.experimental.pallas import tpu as pltpu
from jax.sharding import PartitionSpec as P

STEP = 10


beta_one = 0.9
beta_two = 0.95
epsilon = 1e-08
learn_rate = 0.0003
decay_rate = 0.1
average_keep = 0.999
clip_level = 0.5

MESH = pl.DeviceIdType.MESH
f32 = jnp.float32
bf16 = jnp.bfloat16


def tensor_layout(all_rows, slot_rows, layers):
    layer_rows = all_rows // layers
    kv_rows = (layer_rows - 2 - 2 * slot_rows) // 2
    counts = [slot_rows, kv_rows, kv_rows, slot_rows, 1, 1]
    layout = []
    start = 0
    for layer in range(layers):
        for position, count in enumerate(counts):
            layout.append((start, count, 1.0 if position < 4 else 0.0))
            start = start + count
    return layout


def adam_master(grad, master, moment, second, decay, factor):
    clipped = factor * grad
    moment_new = beta_one * moment + (1.0 - beta_one) * clipped
    second_new = beta_two * second + (1.0 - beta_two) * clipped * clipped
    direction = (
        moment_new
        * (1.0 / (1.0 - beta_one**STEP))
        / (jnp.sqrt(second_new * (1.0 / (1.0 - beta_two**STEP))) + epsilon)
    )
    master_new = master - learn_rate * (direction + decay_rate * decay * master)
    return master_new, moment_new, second_new


def clip_factor(tile, numel):
    squares = jnp.sum(tile, keepdims=True)
    return jnp.minimum(1.0, clip_level / jnp.sqrt(squares / numel + 1e-06))


def fold(x):
    half = x.shape[1] // 2
    return jnp.concatenate([x[:, :half], x[:, half:]], axis=0).astype(bf16)


def unfold(x):
    half = x.shape[0] // 2
    return jnp.concatenate([x[:half], x[half:]], axis=1)


def exchange(
    n, ns, layout, numel,
    grads, owners_hbm, master, moment, second, average,
    w_out, master_out, moment_out, second_out, average_out,
    owners, state, st_send, st_recv, g_mine, g_pair, g_send, g_recv, tot, bk_send, bk_recv, mean_rows, old_rows, w_send, w_recv, q_send, q_recv, s_send, s_recv,
    local_sem, load_sem, pair_sems, g_sems, st_sems, st2_sems, bk_sems, q_sems, s_sems, w_sems, fw_sems,
):
    me = lax.axis_index("dp")
    sec = lax.axis_index("section")
    rows, width = w_out.shape
    cw = width // n
    slot_rows = state.shape[1]
    tensors = len(layout)
    chips = n // 2
    core = lax.rem(me, 2)
    sibling = me + 1 - 2 * core

    def same_core(index, e):
        return lax.rem(index + 2 * e, n)

    def after(d):
        return lax.rem(me + d, n)

    def before(d):
        return lax.rem(me + (n - d), n)

    def cols(index):
        return pl.ds(pl.multiple_of(index * cw, cw), cw)

    loads = [
        pltpu.make_async_copy(ref.at[0, 0], state.at[k], local_sem.at[k])
        for k, ref in enumerate((master, moment, second, average))
    ]
    own_owners = pltpu.make_async_copy(owners_hbm, owners, local_sem.at[4])
    own = [
        pltpu.make_async_copy(
            grads.at[0, 0, :, cols(same_core(me, e))], g_mine.at[e], load_sem.at[e]
        )
        for e in range(chips)
    ]
    for copy in loads + own + [own_owners]:
        copy.start()

    barrier = pltpu.get_barrier_semaphore()
    for d in range(1, n):
        pl.semaphore_signal(barrier, inc=1, device_id={"dp": after(d)}, device_id_type=MESH)
    for e in range(1, ns):
        pl.semaphore_signal(
            barrier, inc=1, device_id={"section": lax.rem(sec + e, ns)}, device_id_type=MESH
        )
    pl.semaphore_wait(barrier, n - 1 + ns - 1)

    def remote(src, dst, sems, d, target):
        copy = pltpu.make_async_remote_copy(
            src_ref=src,
            dst_ref=dst,
            send_sem=sems.at[0, d],
            recv_sem=sems.at[1, d],
            device_id=target,
            device_id_type=MESH,
        )
        copy.start()
        return copy

    pair_copies = [
        remote(
            grads.at[0, 0, :, cols(same_core(sibling, e))], g_pair.at[e], pair_sems, e, {"dp": sibling}
        )
        for e in [*range(1, chips), 0]
    ]

    first = pl.ds(0, 2 * slot_rows)
    others = pl.ds(2 * slot_rows, 4 * slot_rows)
    def pack(k):
        loads[k].wait()
        for d in range(n):
            place = st_recv if d == 0 else st_send
            place[d, 2 * slot_rows * k : 2 * slot_rows * (k + 1), :] = fold(state[k, :, cols(after(d))])

    pack(0)
    st_copies = [
        remote(st_send.at[d, first], st_recv.at[d, first], st_sems, d, {"dp": after(d)})
        for d in range(1, n)
    ]

    for copy in own:
        copy.wait()
    g_copies = []
    for e, copy in zip([*range(1, chips), 0], pair_copies):
        copy.wait_recv()
        pair = g_mine[e].astype(f32) + g_pair[e].astype(f32)
        if e:
            g_send[e] = pair.astype(bf16)
            g_copies.append(
                remote(g_send.at[e], g_recv.at[e], g_sems, e, {"dp": same_core(me, e)})
            )
    pack(1)
    pack(2)
    own_owners.wait()
    total = pair
    for e, copy in zip(range(1, chips), g_copies):
        copy.wait_recv()
        total = total + g_recv[e].astype(f32)
    mean = total / n
    mean_rows[...] = mean
    part = jnp.zeros((slot_rows, 128), f32)
    for r in range(0, rows, slot_rows):
        piece = mean[r : r + slot_rows]
        for c in range(0, cw, 128):
            square = piece[:, c : c + 128] * piece[:, c : c + 128]
            if len(square) < slot_rows:
                lacking = jnp.zeros((slot_rows - len(square), 128), f32)
                square = jnp.concatenate([square, lacking], axis=0)
            part = part + square

    q_send[...] = part
    q_copies = [
        remote(q_send, q_recv.at[d], q_sems, d, {"dp": after(d)}) for d in range(1, n)
    ]

    st_copies += [
        remote(st_send.at[d, others], st_recv.at[d, others], st2_sems, d, {"dp": after(d)})
        for d in range(1, n)
    ]

    for t, (start, count, flag) in enumerate(layout):
        piece = mean_rows[start : start + count, :]
        if count < slot_rows:
            piece = jnp.concatenate([piece, jnp.zeros((slot_rows - count, cw), f32)], axis=0)
        tot[t] = piece
    tot[tensors] = jnp.zeros((slot_rows, cw), f32)

    for d, copy in zip(range(1, n), q_copies):
        copy.wait_recv()
        part = part + q_recv[d]
    s_send[...] = part
    s_copies = [
        remote(s_send, s_recv.at[e], s_sems, e, {"section": lax.rem(sec + e, ns)})
        for e in range(1, ns)
    ]

    bk_copies = []
    for d in range(n):
        target = after(d)
        mine = jnp.int32(tensors)
        for t in range(tensors):
            mine = jnp.where(owners[0, t] == target, t, mine)
        slab = fold(tot[mine])
        if d == 0:
            bk_recv[me] = slab
        else:
            bk_send[d] = slab
            bk_copies.append(
                remote(bk_send.at[d], bk_recv.at[me], bk_sems, d, {"dp": target})
            )

    for copy in st_copies:
        copy.wait_recv()
    row = lax.broadcasted_iota(jnp.int32, (rows, cw), 0)
    decays = jnp.zeros((rows, cw), f32)
    for t, (start, count, flag) in enumerate(layout):
        olds = st_recv[lax.rem(me - owners[0, t] + n, n)].astype(f32)
        for k in range(3):
            old = unfold(olds[2 * slot_rows * k : 2 * slot_rows * (k + 1)])
            old_rows[k, start : start + count, :] = old[:count]
        if flag:
            decays = jnp.where(jnp.logical_and(row >= start, row < start + count), flag, decays)

    for e, copy in zip(range(1, ns), s_copies):
        copy.wait_recv()
        part = part + s_recv[e]
    factor = clip_factor(part, numel)
    fresh, _, _ = adam_master(mean_rows[...], old_rows[0], old_rows[1], old_rows[2], decays, factor)
    w_send[...] = fresh.astype(bf16)
    here = w_out.at[:, cols(me)]
    w_copies = [
        remote(w_send, w_recv.at[e], w_sems, e, {"dp": same_core(me, e)}) for e in range(1, chips)
    ]
    w_copies.append(remote(w_send, here, fw_sems, 0, {"dp": sibling}))
    w_stores = [pltpu.make_async_copy(w_send, here, load_sem.at[0])]
    w_stores[0].start()

    for d in range(1, n):
        place = bk_recv.at[before(d)]
        pltpu.make_async_copy(place, place, bk_sems.at[1, d]).wait()
    loads[3].wait()
    used_rows = jnp.int32(0)
    decay = jnp.float32(0.0)
    for t, (start, count, flag) in enumerate(layout):
        mine = owners[0, t] == me
        used_rows = jnp.where(mine, count, used_rows)
        decay = jnp.where(mine, flag, decay)
    used = lax.broadcasted_iota(jnp.int32, (slot_rows, cw), 0) < used_rows
    for j in range(n):
        at = slice(j * cw, (j + 1) * cw)
        old = [state[k, :, at] for k in range(4)]
        fresh = adam_master(unfold(bk_recv[j].astype(f32)), old[0], old[1], old[2], decay, factor)
        blended = average_keep * old[3] + (1.0 - average_keep) * fresh[0]
        for k, new in enumerate(fresh + (blended,)):
            state[k, :, at] = jnp.where(used, new, old[k])
    stores = [
        pltpu.make_async_copy(state.at[k], ref.at[0, 0], local_sem.at[k])
        for k, ref in enumerate((master_out, moment_out, second_out, average_out))
    ]
    for copy in stores:
        copy.start()

    for copy in pair_copies + g_copies + st_copies + q_copies + s_copies + bk_copies:
        copy.wait_send()

    for e in range(1, chips):
        there = w_out.at[:, cols(same_core(me, chips - e))]
        w_copies[e - 1].wait_recv()
        w_copies.append(remote(w_recv.at[e], there, fw_sems, e, {"dp": sibling}))
        w_stores.append(pltpu.make_async_copy(w_recv.at[e], there, load_sem.at[e]))
        w_stores[-1].start()
    for e in range(chips):
        there = w_out.at[:, cols(same_core(sibling, chips - e))]
        pltpu.make_async_copy(there, there, fw_sems.at[1, e]).wait()
    for copy in w_copies:
        copy.wait_send()
    for copy in stores + w_stores:
        copy.wait()


def hand_out(*refs):
    sources, results, places, sems = refs[:5], refs[5:10], refs[10:15], refs[15]
    loads = [
        pltpu.make_async_copy(source, place, sems.at[0, k])
        for k, (source, place) in enumerate(zip(sources, places))
    ]
    for copy in loads:
        copy.start()
    stores = []
    for k, (place, result) in enumerate(zip(places, results)):
        loads[k].wait()
        stores.append(pltpu.make_async_copy(place, result.at[0] if k == 0 else result, sems.at[1, k]))
        stores[-1].start()
    for copy in stores:
        copy.wait()


def local(grads, owners, master, moment, second, average):
    rows, width = grads.shape[2:]
    slot_rows = master.shape[2]
    n = lax.axis_size("dp")
    ns = lax.axis_size("section")
    cw = width // n
    layout = tensor_layout(rows, slot_rows, owners.shape[1] // 6)
    tensors = len(layout)
    numel = ns * rows * width
    hbm = pl.BlockSpec(memory_space=pl.ANY)
    packed = (n, 2 * slot_rows, cw // 2)
    sems = lambda count: pltpu.SemaphoreType.DMA((2, count))
    state = jax.ShapeDtypeStruct(master.shape, f32)
    results = pl.pallas_call(
        functools.partial(exchange, n, ns, layout, numel),
        out_shape=(jax.ShapeDtypeStruct((rows, width), bf16), state, state, state, state),
        in_specs=[hbm] * 6,
        out_specs=(hbm,) * 5,
        scratch_shapes=[
            pltpu.SMEM(owners.shape, jnp.int32),
            pltpu.VMEM((4, slot_rows, width), f32),
            pltpu.VMEM((n, 6 * slot_rows, cw // 2), bf16),
            pltpu.VMEM((n, 6 * slot_rows, cw // 2), bf16),
            *[pltpu.VMEM((n // 2, rows, cw), bf16)] * 4,
            pltpu.VMEM((tensors + 1, slot_rows, cw), f32),
            pltpu.VMEM(packed, bf16),
            pltpu.VMEM(packed, bf16),
            pltpu.VMEM((rows, cw), f32),
            pltpu.VMEM((3, rows, cw), f32),
            pltpu.VMEM((rows, cw), bf16),
            pltpu.VMEM((n // 2, rows, cw), bf16),
            pltpu.VMEM((slot_rows, 128), f32),
            pltpu.VMEM((n, slot_rows, 128), f32),
            pltpu.VMEM((slot_rows, 128), f32),
            pltpu.VMEM((ns, slot_rows, 128), f32),
            pltpu.SemaphoreType.DMA((5,)),
            pltpu.SemaphoreType.DMA((n // 2,)),
            sems(n // 2), sems(n // 2), sems(n), sems(n), sems(n), sems(n), sems(ns),
            sems(n // 2), sems(n // 2),
        ],
        compiler_params=pltpu.CompilerParams(
            collective_id=0, has_side_effects=True, vmem_limit_bytes=60 * 2**20
        ),
        name="exchange",
    )(grads, owners, master, moment, second, average)
    return pl.pallas_call(
        hand_out,
        out_shape=(jax.ShapeDtypeStruct((1, rows, width), bf16), state, state, state, state),
        in_specs=[hbm] * 5,
        out_specs=(hbm,) * 5,
        scratch_shapes=[
            pltpu.VMEM((rows, width), bf16),
            *[pltpu.VMEM(master.shape, f32)] * 4,
            pltpu.SemaphoreType.DMA((2, 5)),
        ],
        compiler_params=pltpu.CompilerParams(vmem_limit_bytes=60 * 2**20),
        name="hand_out",
    )(*results)


def solution(mesh):
    in_specs = (
        P("section", "dp", None, None),
        P("section", None),
        P("section", "dp", None, None),
        P("section", "dp", None, None),
        P("section", "dp", None, None),
        P("section", "dp", None, None),
    )
    out_specs = (
        P("section", None, None),
        P("section", "dp", None, None),
        P("section", "dp", None, None),
        P("section", "dp", None, None),
        P("section", "dp", None, None),
    )
    return jax.shard_map(local, mesh=mesh, in_specs=in_specs, out_specs=out_specs, check_vma=False)
```

```python
import functools

import jax
import jax.numpy as jnp
from jax import lax
from jax.experimental import pallas as pl
from jax.experimental.pallas import tpu as pltpu
from jax.sharding import PartitionSpec as P

STEP = 10


beta_one = 0.9
beta_two = 0.95
epsilon = 1e-08
learn_rate = 0.0003
decay_rate = 0.1
average_keep = 0.999
clip_level = 0.5

MESH = pl.DeviceIdType.MESH
f32 = jnp.float32
bf16 = jnp.bfloat16


def tensor_layout(all_rows, slot_rows, layers):
    layer_rows = all_rows // layers
    kv_rows = (layer_rows - 2 - 2 * slot_rows) // 2
    counts = [slot_rows, kv_rows, kv_rows, slot_rows, 1, 1]
    layout = []
    start = 0
    for layer in range(layers):
        for position, count in enumerate(counts):
            layout.append((start, count, 1.0 if position < 4 else 0.0))
            start = start + count
    return layout


def adam_master(grad, master, moment, second, decay, factor):
    clipped = factor * grad
    moment_new = beta_one * moment + (1.0 - beta_one) * clipped
    second_new = beta_two * second + (1.0 - beta_two) * clipped * clipped
    direction = (
        moment_new
        * (1.0 / (1.0 - beta_one**STEP))
        / (jnp.sqrt(second_new * (1.0 / (1.0 - beta_two**STEP))) + epsilon)
    )
    master_new = master - learn_rate * (direction + decay_rate * decay * master)
    return master_new, moment_new, second_new


def clip_factor(tile, numel):
    squares = jnp.sum(tile, keepdims=True)
    return jnp.minimum(1.0, clip_level / jnp.sqrt(squares / numel + 1e-06))


def fold(x):
    half = x.shape[1] // 2
    return jnp.concatenate([x[:, :half], x[:, half:]], axis=0).astype(bf16)


def unfold(x):
    half = x.shape[0] // 2
    return jnp.concatenate([x[:half], x[half:]], axis=1)


def exchange(
    n, ns, layout, numel,
    grads, owners_hbm, master, moment, second, average,
    w_out, master_out, moment_out, second_out, average_out,
    owners, state, st_send, st_recv, g_mine, g_pair, g_send, g_recv, tot, bk_send, bk_recv, mean_rows, w_rows, w_send, w_recv, q_send, q_recv, s_send, s_recv,
    local_sem, load_sem, pair_sems, g_sems, st_sems, bk_sems, q_sems, s_sems, w_sems, fw_sems,
):
    me = lax.axis_index("dp")
    sec = lax.axis_index("section")
    rows, width = w_out.shape
    cw = width // n
    slot_rows = state.shape[1]
    tensors = len(layout)
    chips = n // 2
    core = lax.rem(me, 2)
    sibling = me + 1 - 2 * core

    def same_core(index, e):
        return lax.rem(index + 2 * e, n)

    def after(d):
        return lax.rem(me + d, n)

    def before(d):
        return lax.rem(me + (n - d), n)

    def cols(index):
        return pl.ds(pl.multiple_of(index * cw, cw), cw)

    loads = [
        pltpu.make_async_copy(ref.at[0, 0], state.at[k], local_sem.at[k])
        for k, ref in enumerate((master, moment, second, average))
    ]
    own_owners = pltpu.make_async_copy(owners_hbm, owners, local_sem.at[4])
    own = [
        pltpu.make_async_copy(
            grads.at[0, 0, :, cols(same_core(me, e))], g_mine.at[e], load_sem.at[e]
        )
        for e in range(chips)
    ]
    for copy in loads + own + [own_owners]:
        copy.start()

    barrier = pltpu.get_barrier_semaphore()
    for d in range(1, n):
        pl.semaphore_signal(barrier, inc=1, device_id={"dp": after(d)}, device_id_type=MESH)
    for e in range(1, ns):
        pl.semaphore_signal(
            barrier, inc=1, device_id={"section": lax.rem(sec + e, ns)}, device_id_type=MESH
        )
    pl.semaphore_wait(barrier, n - 1 + ns - 1)

    def remote(src, dst, sems, d, target):
        copy = pltpu.make_async_remote_copy(
            src_ref=src,
            dst_ref=dst,
            send_sem=sems.at[0, d],
            recv_sem=sems.at[1, d],
            device_id=target,
            device_id_type=MESH,
        )
        copy.start()
        return copy

    pair_copies = [
        remote(
            grads.at[0, 0, :, cols(same_core(sibling, e))], g_pair.at[e], pair_sems, e, {"dp": sibling}
        )
        for e in [*range(1, chips), 0]
    ]

    for copy in own:
        copy.wait()
    g_copies = []
    for e, copy in zip([*range(1, chips), 0], pair_copies):
        copy.wait_recv()
        pair = g_mine[e].astype(f32) + g_pair[e].astype(f32)
        if e:
            g_send[e] = pair.astype(bf16)
            g_copies.append(
                remote(g_send.at[e], g_recv.at[e], g_sems, e, {"dp": same_core(me, e)})
            )
    own_owners.wait()
    total = pair
    for e, copy in zip(range(1, chips), g_copies):
        copy.wait_recv()
        total = total + g_recv[e].astype(f32)
    mean = total / n
    mean_rows[...] = mean
    part = jnp.zeros((slot_rows, 128), f32)
    for r in range(0, rows, slot_rows):
        piece = mean[r : r + slot_rows]
        for c in range(0, cw, 128):
            square = piece[:, c : c + 128] * piece[:, c : c + 128]
            if len(square) < slot_rows:
                lacking = jnp.zeros((slot_rows - len(square), 128), f32)
                square = jnp.concatenate([square, lacking], axis=0)
            part = part + square

    q_send[...] = part
    q_copies = [
        remote(q_send, q_recv.at[d], q_sems, d, {"dp": after(d)}) for d in range(1, n)
    ]

    for t, (start, count, flag) in enumerate(layout):
        piece = mean_rows[start : start + count, :]
        if count < slot_rows:
            piece = jnp.concatenate([piece, jnp.zeros((slot_rows - count, cw), f32)], axis=0)
        tot[t] = piece
    tot[tensors] = jnp.zeros((slot_rows, cw), f32)

    bk_copies = []
    for d in range(n):
        target = after(d)
        mine = jnp.int32(tensors)
        for t in range(tensors):
            mine = jnp.where(owners[0, t] == target, t, mine)
        slab = fold(tot[mine])
        if d == 0:
            bk_recv[me] = slab
        else:
            bk_send[d] = slab
            bk_copies.append(
                remote(bk_send.at[d], bk_recv.at[me], bk_sems, d, {"dp": target})
            )

    for d, copy in zip(range(1, n), q_copies):
        copy.wait_recv()
        part = part + q_recv[d]
    s_send[...] = part
    s_copies = [
        remote(s_send, s_recv.at[e], s_sems, e, {"section": lax.rem(sec + e, ns)})
        for e in range(1, ns)
    ]

    for copy in loads:
        copy.wait()
    for d in range(1, n):
        place = bk_recv.at[before(d)]
        pltpu.make_async_copy(place, place, bk_sems.at[1, d]).wait()
    used_rows = jnp.int32(0)
    decay = jnp.float32(0.0)
    for t, (start, count, flag) in enumerate(layout):
        mine = owners[0, t] == me
        used_rows = jnp.where(mine, count, used_rows)
        decay = jnp.where(mine, flag, decay)
    used = lax.broadcasted_iota(jnp.int32, (slot_rows, cw), 0) < used_rows

    for e, copy in zip(range(1, ns), s_copies):
        copy.wait_recv()
        part = part + s_recv[e]
    factor = clip_factor(part, numel)

    st_copies = []
    for d in [*range(1, n), 0]:
        at = cols(after(d))
        old = [state[k, :, at] for k in range(4)]
        grad = unfold(bk_recv[after(d)].astype(f32))
        fresh = adam_master(grad, old[0], old[1], old[2], decay, factor)
        blended = average_keep * old[3] + (1.0 - average_keep) * fresh[0]
        kept = [jnp.where(used, new, o) for new, o in zip(fresh + (blended,), old)]
        if d:
            st_send[d] = fold(kept[0])
            st_copies.append(remote(st_send.at[d], st_recv.at[d], st_sems, d, {"dp": after(d)}))
        else:
            st_recv[0] = fold(kept[0])
        for k in range(4):
            state[k, :, at] = kept[k]
    stores = [
        pltpu.make_async_copy(state.at[k], ref.at[0, 0], local_sem.at[k])
        for k, ref in enumerate((master_out, moment_out, second_out, average_out))
    ]
    for copy in stores:
        copy.start()
    for copy in st_copies:
        copy.wait_recv()
    for t, (start, count, flag) in enumerate(layout):
        block = unfold(st_recv[lax.rem(me - owners[0, t] + n, n)].astype(f32))
        w_rows[start : start + count, :] = block[:count]
    w_send[...] = w_rows[...].astype(bf16)
    here = w_out.at[:, cols(me)]
    w_copies = [
        remote(w_send, w_recv.at[e], w_sems, e, {"dp": same_core(me, e)}) for e in range(1, chips)
    ]
    w_copies.append(remote(w_send, here, fw_sems, 0, {"dp": sibling}))
    w_stores = [pltpu.make_async_copy(w_send, here, load_sem.at[0])]
    w_stores[0].start()

    for copy in pair_copies + g_copies + st_copies + q_copies + s_copies + bk_copies:
        copy.wait_send()

    for e in range(1, chips):
        there = w_out.at[:, cols(same_core(me, chips - e))]
        w_copies[e - 1].wait_recv()
        w_copies.append(remote(w_recv.at[e], there, fw_sems, e, {"dp": sibling}))
        w_stores.append(pltpu.make_async_copy(w_recv.at[e], there, load_sem.at[e]))
        w_stores[-1].start()
    for e in range(chips):
        there = w_out.at[:, cols(same_core(sibling, chips - e))]
        pltpu.make_async_copy(there, there, fw_sems.at[1, e]).wait()
    for copy in w_copies:
        copy.wait_send()
    for copy in stores + w_stores:
        copy.wait()


def hand_out(*refs):
    sources, results, places, sems = refs[:5], refs[5:10], refs[10:15], refs[15]
    loads = [
        pltpu.make_async_copy(source, place, sems.at[0, k])
        for k, (source, place) in enumerate(zip(sources, places))
    ]
    for copy in loads:
        copy.start()
    stores = []
    for k, (place, result) in enumerate(zip(places, results)):
        loads[k].wait()
        stores.append(pltpu.make_async_copy(place, result.at[0] if k == 0 else result, sems.at[1, k]))
        stores[-1].start()
    for copy in stores:
        copy.wait()


def local(grads, owners, master, moment, second, average):
    rows, width = grads.shape[2:]
    slot_rows = master.shape[2]
    n = lax.axis_size("dp")
    ns = lax.axis_size("section")
    cw = width // n
    layout = tensor_layout(rows, slot_rows, owners.shape[1] // 6)
    tensors = len(layout)
    numel = ns * rows * width
    hbm = pl.BlockSpec(memory_space=pl.ANY)
    packed = (n, 2 * slot_rows, cw // 2)
    sems = lambda count: pltpu.SemaphoreType.DMA((2, count))
    state = jax.ShapeDtypeStruct(master.shape, f32)
    results = pl.pallas_call(
        functools.partial(exchange, n, ns, layout, numel),
        out_shape=(jax.ShapeDtypeStruct((rows, width), bf16), state, state, state, state),
        in_specs=[hbm] * 6,
        out_specs=(hbm,) * 5,
        scratch_shapes=[
            pltpu.SMEM(owners.shape, jnp.int32),
            pltpu.VMEM((4, slot_rows, width), f32),
            pltpu.VMEM(packed, bf16),
            pltpu.VMEM(packed, bf16),
            *[pltpu.VMEM((n // 2, rows, cw), bf16)] * 4,
            pltpu.VMEM((tensors + 1, slot_rows, cw), f32),
            pltpu.VMEM(packed, bf16),
            pltpu.VMEM(packed, bf16),
            pltpu.VMEM((rows, cw), f32),
            pltpu.VMEM((rows, cw), f32),
            pltpu.VMEM((rows, cw), bf16),
            pltpu.VMEM((n // 2, rows, cw), bf16),
            pltpu.VMEM((slot_rows, 128), f32),
            pltpu.VMEM((n, slot_rows, 128), f32),
            pltpu.VMEM((slot_rows, 128), f32),
            pltpu.VMEM((ns, slot_rows, 128), f32),
            pltpu.SemaphoreType.DMA((5,)),
            pltpu.SemaphoreType.DMA((n // 2,)),
            sems(n // 2), sems(n // 2), sems(n), sems(n), sems(n), sems(ns),
            sems(n // 2), sems(n // 2),
        ],
        compiler_params=pltpu.CompilerParams(
            collective_id=0, has_side_effects=True, vmem_limit_bytes=60 * 2**20
        ),
        name="exchange",
    )(grads, owners, master, moment, second, average)
    return pl.pallas_call(
        hand_out,
        out_shape=(jax.ShapeDtypeStruct((1, rows, width), bf16), state, state, state, state),
        in_specs=[hbm] * 5,
        out_specs=(hbm,) * 5,
        scratch_shapes=[
            pltpu.VMEM((rows, width), bf16),
            *[pltpu.VMEM(master.shape, f32)] * 4,
            pltpu.SemaphoreType.DMA((2, 5)),
        ],
        compiler_params=pltpu.CompilerParams(vmem_limit_bytes=60 * 2**20),
        name="hand_out",
    )(*results)


def solution(mesh):
    in_specs = (
        P("section", "dp", None, None),
        P("section", None),
        P("section", "dp", None, None),
        P("section", "dp", None, None),
        P("section", "dp", None, None),
        P("section", "dp", None, None),
    )
    out_specs = (
        P("section", None, None),
        P("section", "dp", None, None),
        P("section", "dp", None, None),
        P("section", "dp", None, None),
        P("section", "dp", None, None),
    )
    return jax.shard_map(local, mesh=mesh, in_specs=in_specs, out_specs=out_specs, check_vma=False)
```

```python
import functools

import jax
import jax.numpy as jnp
from jax import lax
from jax.experimental import pallas as pl
from jax.experimental.pallas import tpu as pltpu
from jax.sharding import PartitionSpec as P

STEP = 10


beta_one = 0.9
beta_two = 0.95
epsilon = 1e-08
learn_rate = 0.0003
decay_rate = 0.1
average_keep = 0.999
clip_level = 0.5

MESH = pl.DeviceIdType.MESH
f32 = jnp.float32
bf16 = jnp.bfloat16


def tensor_layout(all_rows, slot_rows, layers):
    layer_rows = all_rows // layers
    kv_rows = (layer_rows - 2 - 2 * slot_rows) // 2
    counts = [slot_rows, kv_rows, kv_rows, slot_rows, 1, 1]
    layout = []
    start = 0
    for layer in range(layers):
        for position, count in enumerate(counts):
            layout.append((start, count, 1.0 if position < 4 else 0.0))
            start = start + count
    return layout


def adam_master(grad, master, moment, second, decay, factor):
    clipped = factor * grad
    moment_new = beta_one * moment + (1.0 - beta_one) * clipped
    second_new = beta_two * second + (1.0 - beta_two) * clipped * clipped
    direction = (
        moment_new
        * (1.0 / (1.0 - beta_one**STEP))
        / (jnp.sqrt(second_new * (1.0 / (1.0 - beta_two**STEP))) + epsilon)
    )
    master_new = master - learn_rate * (direction + decay_rate * decay * master)
    return master_new, moment_new, second_new


def clip_factor(tile, numel):
    squares = jnp.sum(tile, keepdims=True)
    return jnp.minimum(1.0, clip_level / jnp.sqrt(squares / numel + 1e-06))


def fold(x):
    half = x.shape[1] // 2
    return jnp.concatenate([x[:, :half], x[:, half:]], axis=0).astype(bf16)


def unfold(x):
    half = x.shape[0] // 2
    return jnp.concatenate([x[:half], x[half:]], axis=1)


def exchange(
    n, ns, layout, numel,
    grads, owners_hbm, master, moment, second, average,
    w_out, master_out, moment_out, second_out, average_out,
    owners, state, st_send, st_recv, g_mine, g_pair, g_send, g_recv, tot, bk_send, bk_recv, mean_rows, old_rows, w_send, w_recv, q_send, q_recv,
    local_sem, load_sem, pair_sems, g_sems, st_sems, st2_sems, bk_sems, q_sems, w_sems, fw_sems,
):
    me = lax.axis_index("dp")
    sec = lax.axis_index("section")
    rows, width = w_out.shape
    cw = width // n
    slot_rows = state.shape[1]
    tensors = len(layout)
    chips = n // 2
    core = lax.rem(me, 2)
    sibling = me + 1 - 2 * core

    def same_core(index, e):
        return lax.rem(index + 2 * e, n)

    def after(d):
        return lax.rem(me + d, n)

    def before(d):
        return lax.rem(me + (n - d), n)

    def cols(index):
        return pl.ds(pl.multiple_of(index * cw, cw), cw)

    loads = [
        pltpu.make_async_copy(ref.at[0, 0], state.at[k], local_sem.at[k])
        for k, ref in enumerate((master, moment, second, average))
    ]
    own_owners = pltpu.make_async_copy(owners_hbm, owners, local_sem.at[4])
    own = [
        pltpu.make_async_copy(
            grads.at[0, 0, :, cols(same_core(me, e))], g_mine.at[e], load_sem.at[e]
        )
        for e in range(chips)
    ]
    for copy in loads + own + [own_owners]:
        copy.start()

    barrier = pltpu.get_barrier_semaphore()
    def other(i):
        return {"section": lax.rem(sec + i // n, ns), "dp": lax.rem(me + i % n, n)}

    @pl.loop(1, n * ns)
    def _(i):
        pl.semaphore_signal(barrier, inc=1, device_id=other(i), device_id_type=MESH)

    pl.semaphore_wait(barrier, n * ns - 1)

    def remote(src, dst, sems, d, target):
        copy = pltpu.make_async_remote_copy(
            src_ref=src,
            dst_ref=dst,
            send_sem=sems.at[0, d],
            recv_sem=sems.at[1, d],
            device_id=target,
            device_id_type=MESH,
        )
        copy.start()
        return copy

    pair_copies = [
        remote(
            grads.at[0, 0, :, cols(same_core(sibling, e))], g_pair.at[e], pair_sems, e, {"dp": sibling}
        )
        for e in [*range(1, chips), 0]
    ]

    first = pl.ds(0, 2 * slot_rows)
    others = pl.ds(2 * slot_rows, 4 * slot_rows)
    def pack(k):
        loads[k].wait()
        for d in range(n):
            place = st_recv if d == 0 else st_send
            place[d, 2 * slot_rows * k : 2 * slot_rows * (k + 1), :] = fold(state[k, :, cols(after(d))])

    pack(0)
    st_copies = [
        remote(st_send.at[d, first], st_recv.at[d, first], st_sems, d, {"dp": after(d)})
        for d in range(1, n)
    ]

    for copy in own:
        copy.wait()
    g_copies = []
    for e, copy in zip([*range(1, chips), 0], pair_copies):
        copy.wait_recv()
        pair = g_mine[e].astype(f32) + g_pair[e].astype(f32)
        if e:
            g_send[e] = pair.astype(bf16)
            g_copies.append(
                remote(g_send.at[e], g_recv.at[e], g_sems, e, {"dp": same_core(me, e)})
            )
    pack(1)
    pack(2)
    own_owners.wait()
    total = pair
    for e, copy in zip(range(1, chips), g_copies):
        copy.wait_recv()
        total = total + g_recv[e].astype(f32)
    mean = total / n
    mean_rows[...] = mean
    part = jnp.zeros((slot_rows, 128), f32)
    for r in range(0, rows, slot_rows):
        piece = mean[r : r + slot_rows]
        for c in range(0, cw, 128):
            square = piece[:, c : c + 128] * piece[:, c : c + 128]
            if len(square) < slot_rows:
                lacking = jnp.zeros((slot_rows - len(square), 128), f32)
                square = jnp.concatenate([square, lacking], axis=0)
            part = part + square

    q_send[...] = part

    def square_copy(i):
        return pltpu.make_async_remote_copy(
            src_ref=q_send,
            dst_ref=q_recv.at[i],
            send_sem=q_sems.at[0],
            recv_sem=q_sems.at[1],
            device_id=other(i),
            device_id_type=MESH,
        )

    @pl.loop(1, n * ns)
    def _(i):
        square_copy(i).start()

    st_copies += [
        remote(st_send.at[d, others], st_recv.at[d, others], st2_sems, d, {"dp": after(d)})
        for d in range(1, n)
    ]

    for t, (start, count, flag) in enumerate(layout):
        piece = mean_rows[start : start + count, :]
        if count < slot_rows:
            piece = jnp.concatenate([piece, jnp.zeros((slot_rows - count, cw), f32)], axis=0)
        tot[t] = piece
    tot[tensors] = jnp.zeros((slot_rows, cw), f32)

    bk_copies = []
    for d in range(n):
        target = after(d)
        mine = jnp.int32(tensors)
        for t in range(tensors):
            mine = jnp.where(owners[0, t] == target, t, mine)
        slab = fold(tot[mine])
        if d == 0:
            bk_recv[me] = slab
        else:
            bk_send[d] = slab
            bk_copies.append(
                remote(bk_send.at[d], bk_recv.at[me], bk_sems, d, {"dp": target})
            )

    for copy in st_copies:
        copy.wait_recv()
    row = lax.broadcasted_iota(jnp.int32, (rows, cw), 0)
    decays = jnp.zeros((rows, cw), f32)
    for t, (start, count, flag) in enumerate(layout):
        olds = st_recv[lax.rem(me - owners[0, t] + n, n)].astype(f32)
        for k in range(3):
            old = unfold(olds[2 * slot_rows * k : 2 * slot_rows * (k + 1)])
            old_rows[k, start : start + count, :] = old[:count]
        if flag:
            decays = jnp.where(jnp.logical_and(row >= start, row < start + count), flag, decays)

    arrived = q_recv.at[pl.ds(1, n * ns - 1)]
    pltpu.make_async_copy(arrived, arrived, q_sems.at[1]).wait()
    part = part + jnp.sum(q_recv[1:], axis=0)
    factor = clip_factor(part, numel)
    fresh, _, _ = adam_master(mean_rows[...], old_rows[0], old_rows[1], old_rows[2], decays, factor)
    w_send[...] = fresh.astype(bf16)
    here = w_out.at[:, cols(me)]
    w_copies = [
        remote(w_send, w_recv.at[e], w_sems, e, {"dp": same_core(me, e)}) for e in range(1, chips)
    ]
    w_copies.append(remote(w_send, here, fw_sems, 0, {"dp": sibling}))
    w_stores = [pltpu.make_async_copy(w_send, here, load_sem.at[0])]
    w_stores[0].start()

    for d in range(1, n):
        place = bk_recv.at[before(d)]
        pltpu.make_async_copy(place, place, bk_sems.at[1, d]).wait()
    loads[3].wait()
    used_rows = jnp.int32(0)
    decay = jnp.float32(0.0)
    for t, (start, count, flag) in enumerate(layout):
        mine = owners[0, t] == me
        used_rows = jnp.where(mine, count, used_rows)
        decay = jnp.where(mine, flag, decay)
    used = lax.broadcasted_iota(jnp.int32, (slot_rows, cw), 0) < used_rows
    for j in range(n):
        at = slice(j * cw, (j + 1) * cw)
        old = [state[k, :, at] for k in range(4)]
        fresh = adam_master(unfold(bk_recv[j].astype(f32)), old[0], old[1], old[2], decay, factor)
        blended = average_keep * old[3] + (1.0 - average_keep) * fresh[0]
        for k, new in enumerate(fresh + (blended,)):
            state[k, :, at] = jnp.where(used, new, old[k])
    stores = [
        pltpu.make_async_copy(state.at[k], ref.at[0, 0], local_sem.at[k])
        for k, ref in enumerate((master_out, moment_out, second_out, average_out))
    ]
    for copy in stores:
        copy.start()

    for copy in pair_copies + g_copies + st_copies + bk_copies:
        copy.wait_send()
    pltpu.make_async_copy(arrived, arrived, q_sems.at[0]).wait()

    for e in range(1, chips):
        there = w_out.at[:, cols(same_core(me, chips - e))]
        w_copies[e - 1].wait_recv()
        w_copies.append(remote(w_recv.at[e], there, fw_sems, e, {"dp": sibling}))
        w_stores.append(pltpu.make_async_copy(w_recv.at[e], there, load_sem.at[e]))
        w_stores[-1].start()
    for e in range(chips):
        there = w_out.at[:, cols(same_core(sibling, chips - e))]
        pltpu.make_async_copy(there, there, fw_sems.at[1, e]).wait()
    for copy in w_copies:
        copy.wait_send()
    for copy in stores + w_stores:
        copy.wait()


def hand_out(*refs):
    sources, results, places, sems = refs[:5], refs[5:10], refs[10:15], refs[15]
    loads = [
        pltpu.make_async_copy(source, place, sems.at[0, k])
        for k, (source, place) in enumerate(zip(sources, places))
    ]
    for copy in loads:
        copy.start()
    stores = []
    for k, (place, result) in enumerate(zip(places, results)):
        loads[k].wait()
        stores.append(pltpu.make_async_copy(place, result.at[0] if k == 0 else result, sems.at[1, k]))
        stores[-1].start()
    for copy in stores:
        copy.wait()


def local(grads, owners, master, moment, second, average):
    rows, width = grads.shape[2:]
    slot_rows = master.shape[2]
    n = lax.axis_size("dp")
    ns = lax.axis_size("section")
    cw = width // n
    layout = tensor_layout(rows, slot_rows, owners.shape[1] // 6)
    tensors = len(layout)
    numel = ns * rows * width
    hbm = pl.BlockSpec(memory_space=pl.ANY)
    packed = (n, 2 * slot_rows, cw // 2)
    sems = lambda count: pltpu.SemaphoreType.DMA((2, count))
    state = jax.ShapeDtypeStruct(master.shape, f32)
    results = pl.pallas_call(
        functools.partial(exchange, n, ns, layout, numel),
        out_shape=(jax.ShapeDtypeStruct((rows, width), bf16), state, state, state, state),
        in_specs=[hbm] * 6,
        out_specs=(hbm,) * 5,
        scratch_shapes=[
            pltpu.SMEM(owners.shape, jnp.int32),
            pltpu.VMEM((4, slot_rows, width), f32),
            pltpu.VMEM((n, 6 * slot_rows, cw // 2), bf16),
            pltpu.VMEM((n, 6 * slot_rows, cw // 2), bf16),
            *[pltpu.VMEM((n // 2, rows, cw), bf16)] * 4,
            pltpu.VMEM((tensors + 1, slot_rows, cw), f32),
            pltpu.VMEM(packed, bf16),
            pltpu.VMEM(packed, bf16),
            pltpu.VMEM((rows, cw), f32),
            pltpu.VMEM((3, rows, cw), f32),
            pltpu.VMEM((rows, cw), bf16),
            pltpu.VMEM((n // 2, rows, cw), bf16),
            pltpu.VMEM((slot_rows, 128), f32),
            pltpu.VMEM((n * ns, slot_rows, 128), f32),
            pltpu.SemaphoreType.DMA((5,)),
            pltpu.SemaphoreType.DMA((n // 2,)),
            sems(n // 2), sems(n // 2), sems(n), sems(n), sems(n), pltpu.SemaphoreType.DMA((2,)),
            sems(n // 2), sems(n // 2),
        ],
        compiler_params=pltpu.CompilerParams(
            collective_id=0, has_side_effects=True, vmem_limit_bytes=60 * 2**20
        ),
        name="exchange",
    )(grads, owners, master, moment, second, average)
    return pl.pallas_call(
        hand_out,
        out_shape=(jax.ShapeDtypeStruct((1, rows, width), bf16), state, state, state, state),
        in_specs=[hbm] * 5,
        out_specs=(hbm,) * 5,
        scratch_shapes=[
            pltpu.VMEM((rows, width), bf16),
            *[pltpu.VMEM(master.shape, f32)] * 4,
            pltpu.SemaphoreType.DMA((2, 5)),
        ],
        compiler_params=pltpu.CompilerParams(vmem_limit_bytes=60 * 2**20),
        name="hand_out",
    )(*results)


def solution(mesh):
    in_specs = (
        P("section", "dp", None, None),
        P("section", None),
        P("section", "dp", None, None),
        P("section", "dp", None, None),
        P("section", "dp", None, None),
        P("section", "dp", None, None),
    )
    out_specs = (
        P("section", None, None),
        P("section", "dp", None, None),
        P("section", "dp", None, None),
        P("section", "dp", None, None),
        P("section", "dp", None, None),
    )
    return jax.shard_map(local, mesh=mesh, in_specs=in_specs, out_specs=out_specs, check_vma=False)
```
